512 devices in a mesh: row: 16 (over z_hi, y, core), col: 32 (over z_lo, x).
Axes of the slice: x: 4, y: 4, z: 16 (z_hi: 2, z_lo: 8; z = z_hi * 8 + z_lo), core: 2. Of those that a mesh axis runs over, the one named last changes fastest.
Arguments:
- gradient: bfloat16 [3584, 3584], P('row', 'col'), may hold values from -6 to 6
- moment: float32 [3584, 3584], P('row', 'col'), may hold values from -1.5 to 1.5
- second: float32 [3584, 3584], P('row', 'col'), may hold values from 0.001 to 0.3
- left_factor: float32 [3584, 3584], P('row', 'col'), may hold values from -6 to 6
- right_factor: float32 [3584, 3584], P('row', 'col'), may hold values from -6 to 6
- left_basis_t: bfloat16 [3584, 3584], P('row', 'col'), may hold values from -0.09375 to 0.09375
- right_basis: bfloat16 [3584, 3584], P('row', 'col'), may hold values from -0.09375 to 0.09375
Outputs:
- left_out: float32 [3584, 3584], P('row', 'col')
- right_out: float32 [3584, 3584], P('row', 'col')
- moment_out: float32 [3584, 3584], P('row', 'col')
- second_out: float32 [3584, 3584], P('row', 'col')
- update: bfloat16 [3584, 3584], P('row', 'col')
The draws below stay inside these ranges and needn't reach their ends.
All inputs are finite; a program needn't handle non-finite values.
Results may differ from the reference program's by a relative error of at most 0.03.
Values may be sent and summed in bfloat16 or wider, within the bound.
A program may use at most 64 MiB of HBM per device.

```python
import math
import jax
import jax.numpy as jnp
from jax import lax

D = 3584
N_ROW = 16
N_COL = 32


def block_levels(stream_key, dims, pieces, low, high):
    def one(dim, blocks):
        draws = jax.random.uniform(jax.random.fold_in(jax.random.fold_in(stream_key, 6), dim), (blocks,), jnp.float32, low / len(pieces), high / len(pieces))
        return jnp.repeat(jnp.exp(draws), dims[dim] // blocks).reshape((-1,) + (1,) * (len(dims) - dim - 1))

    level = one(*pieces[0])
    for cut in pieces[1:]:
        level = level * one(*cut)
    return level


def normal_values(own_key, shape, deviation, most, split=(), held_as=jnp.bfloat16):
    array = deviation * jax.random.normal(own_key, shape, jnp.float32)
    if split:
        array = array * block_levels(own_key, shape, split, -0.22, 0.18)
    return jnp.clip(array, -most, most).astype(held_as)


def setup_inputs(seed: int = 0) -> dict:
    streams_of = jax.random.split(jax.random.key(seed), 8)
    return {
        "gradient": normal_values(streams_of[0], (D, D), 1.0, 6.0, ((0, 16), (1, 32))),
        "moment": normal_values(streams_of[1], (D, D), 0.1, 1.5, ((0, 16), (1, 32)), jnp.float32),
        "second": jnp.clip(jnp.exp(math.log(0.3) - 5.7037825 * jax.random.uniform(streams_of[2], (D, D), jnp.float32) ** block_levels(streams_of[2], (D, D), ((0, 16), (1, 32)), -0.2, 0.2)), 0.001, 0.3),
        "left_factor": normal_values(streams_of[3], (D, D), 1.0, 6.0, ((0, 16), (1, 32)), jnp.float32),
        "right_factor": normal_values(streams_of[4], (D, D), 1.0, 6.0, ((0, 16), (1, 32)), jnp.float32),
        "left_basis_t": normal_values(streams_of[5], (D, D), D ** -0.5, 0.09375, ((0, 16), (1, 32))),
        "right_basis": normal_values(streams_of[6], (D, D), D ** -0.5, 0.09375, ((0, 16), (1, 32))),
    }


beta_moment = 0.9
beta_second = 0.95
beta_factor = 0.95
epsilon = 1e-08

def add_rounded(running, term):
    term = lax.optimization_barrier(term.astype(jnp.bfloat16))
    return running + term.astype(jnp.float32)

def reference(gradient, moment, second, left_factor, right_factor, left_basis_t, right_basis):
    moment_out = beta_moment * moment + (1.0 - beta_moment) * gradient.astype(jnp.float32)
    moment_half = moment_out.astype(jnp.bfloat16)
    left_out = beta_factor * left_factor + (1.0 - beta_factor) * jnp.dot(gradient, gradient.T, preferred_element_type=jnp.float32)
    right_out = beta_factor * right_factor + (1.0 - beta_factor) * jnp.dot(gradient.T, gradient, preferred_element_type=jnp.float32)
    inner_grad = jnp.dot(left_basis_t, gradient, preferred_element_type=jnp.float32).astype(jnp.bfloat16)
    inner_moment = jnp.dot(left_basis_t, moment_half, preferred_element_type=jnp.float32).astype(jnp.bfloat16)
    grad_rot = jnp.dot(inner_grad, right_basis, preferred_element_type=jnp.float32)
    moment_rot = jnp.dot(inner_moment, right_basis, preferred_element_type=jnp.float32)
    second_out = beta_second * second + (1.0 - beta_second) * grad_rot * grad_rot
    direction = (moment_rot / (jnp.sqrt(second_out) + epsilon)).astype(jnp.bfloat16)
    row_block = D // N_ROW
    basis_blocks = left_basis_t.reshape(N_ROW, row_block, D)
    direction_blocks = direction.reshape(N_ROW, row_block, D)

    def left_step(running, pair):
        term = jnp.dot(pair[0].T, pair[1], preferred_element_type=jnp.float32)
        return (add_rounded(running, term), None)
    back_sum, ignored = lax.scan(left_step, jnp.zeros((D, D), jnp.float32), (basis_blocks, direction_blocks))
    back_left = back_sum.astype(jnp.bfloat16)
    col_block = D // N_COL
    back_blocks = back_left.reshape(D, N_COL, col_block).transpose(1, 0, 2)
    right_blocks = right_basis.reshape(D, N_COL, col_block).transpose(1, 0, 2)

    def right_step(running, pair):
        term = jnp.dot(pair[0], pair[1].T, preferred_element_type=jnp.float32)
        return (add_rounded(running, term), None)
    update_sum, ignored = lax.scan(right_step, jnp.zeros((D, D), jnp.float32), (back_blocks, right_blocks))
    update = update_sum.astype(jnp.bfloat16)
    return (left_out, right_out, moment_out, second_out, update)
```

```python
import functools

import jax
import jax.numpy as jnp
from jax import lax
from jax.experimental import pallas as pl
from jax.experimental.pallas import tpu as pltpu
from jax.sharding import PartitionSpec as P

beta_moment = 0.9
beta_second = 0.95
beta_factor = 0.95
epsilon = 1e-08

MESH = pl.DeviceIdType.MESH
LANES = 128
BF16 = jnp.bfloat16
F32 = jnp.float32
DIMS = (2, 4, 2, 8, 4)


def run(*steps):
    live = list(steps)
    while live:
        for one in list(live):
            try:
                next(one)
            except StopIteration:
                live.remove(one)


def both(first, second):
    if first is None:
        return second
    if second is None:
        return first
    return jnp.logical_and(first, second)


def when(condition, action):
    if condition is None:
        action()
    else:
        pl.when(condition)(action)


def kernel(
    dims, g_ref, m_ref, sec_ref, lf_ref, rf_ref, l_ref, r_ref,
    lo_ref, ro_ref, mo_ref, so_ref, up_ref,
    gm, lb, rb, hb, bt, bt_core, bt_half, bt_full, bt_zs, bt_zr, bt_acc,
    gt, gt_core, gt_half, gt_full, gt_zs, gt_zr, gt_acc,
    ut, ut_half, ut_full, ut_zs, ut_zu, ut_zd, ut_acc, part, turn, facing,
    ssem, rsem,
):
    ZH, Y, CORE, ZL, X = dims
    R, C = ZH * Y * CORE, ZL * X
    rows, cols = g_ref.shape
    row, col = lax.axis_index("row"), lax.axis_index("col")
    core, y, zh = row % CORE, (row // CORE) % Y, row // (CORE * Y)
    x, z = col % X, col // X

    def at_row(zh_, y_, core_):
        return ((zh_ * Y + y_) * CORE + core_, col)

    def at_col(z_, x_):
        return (row, z_ * X + x_)

    y_up, y_dn, y_far = (y + 1) % Y, (y + Y - 1) % Y, (y + 2) % Y
    x_up, x_dn, x_far = (x + 1) % X, (x + X - 1) % X, (x + 2) % X
    to_y_up, to_y_dn = at_row(zh, y_up, core), at_row(zh, y_dn, core)
    to_zh, to_core = at_row(1 - zh, y, core), at_row(zh, y, 1 - core)
    to_x_up, to_x_dn = at_col(z, x_up), at_col(z, x_dn)
    to_z_up, to_z_dn = at_col(z + 1, x), at_col(z - 1, x)
    some = to_x_up if X > 1 else to_core if CORE > 1 else to_y_up

    counts = {"send": 0, "recv": 0}

    def sems(kind, number):
        first = counts[kind]
        counts[kind] += number
        return first

    pending = []

    def send(source, target, s, r, device, condition=None):
        copy = pltpu.make_async_remote_copy(
            src_ref=source, dst_ref=target, send_sem=ssem.at[s], recv_sem=rsem.at[r],
            device_id=device, device_id_type=MESH,
        )
        when(condition, copy.start)
        pending.append((condition, copy))

    def arrive(target, r, condition=None):
        copy = pltpu.make_async_remote_copy(
            src_ref=target, dst_ref=target, send_sem=ssem.at[0], recv_sem=rsem.at[r],
            device_id=some, device_id_type=MESH,
        )
        when(condition, copy.wait_recv)

    def gather_cols(buf):
        half = buf.shape[1] // 2
        low, high = pl.ds(0, half), pl.ds(half, half)
        sz, rz = sems("send", 2 * ZL), sems("recv", ZL)
        sx, rx = sems("send", 4 * ZL), sems("recv", 4 * ZL)

        def slot(z_, x_):
            return z_ * X + x_

        def items(t):
            if t == 0:
                return [(z, None, 0)]
            return [(z - t, z >= t, 1), (z + t, z + t < ZL, -1)]

        def turn_corner(t):
            if X == 1:
                return
            for zo, ok, _ in items(t):
                arrive(buf.at[slot(zo, x_dn)], rx + 4 * zo, ok)
                send(buf.at[slot(zo, x_dn), low], buf.at[slot(zo, x_dn), low],
                     sx + 4 * zo + 2, rx + 4 * zo + 2, to_x_up, ok)
                arrive(buf.at[slot(zo, x_up)], rx + 4 * zo + 1, ok)
                send(buf.at[slot(zo, x_up), high], buf.at[slot(zo, x_up), high],
                     sx + 4 * zo + 3, rx + 4 * zo + 3, to_x_dn, ok)

        for t in range(ZL):
            for zo, ok, way in items(t):
                here = buf.at[slot(zo, x)]
                if t > 0:
                    arrive(here, rz + zo, ok)
                if way >= 0 and t < ZL - 1:
                    send(here, here, sz + zo, rz + zo, to_z_up, both(ok, z < ZL - 1))
                if way <= 0 and t < ZL - 1:
                    send(here, here, sz + ZL + zo, rz + zo, to_z_dn, both(ok, z > 0))
                if X > 1:
                    send(here, here, sx + 4 * zo, rx + 4 * zo, to_x_up, ok)
                    send(here, here, sx + 4 * zo + 1, rx + 4 * zo + 1, to_x_dn, ok)
            yield
            if t > 0:
                turn_corner(t - 1)
                yield
        turn_corner(ZL - 1)
        yield
        if X > 1:
            for zo in range(ZL):
                arrive(buf.at[slot(zo, x_far), low], rx + 4 * zo + 2)
                arrive(buf.at[slot(zo, x_far), high], rx + 4 * zo + 3)
            yield

    def gather_rows(buf):
        half = buf.shape[3] // 2
        low, high = pl.ds(0, half), pl.ds(half, half)
        sz, rz = sems("send", 1), sems("recv", 1)
        sy, ry = sems("send", 4 * ZH), sems("recv", 4 * ZH)
        sc, rc = sems("send", ZH), sems("recv", ZH)
        levels = [zh, 1 - zh][:ZH]
        here = buf.at[core, zh, y]
        if ZH > 1:
            send(here, here, sz, rz, to_zh)
        for k, zi in enumerate(levels):
            mine = buf.at[core, zi, y]
            if k == 1:
                yield
                arrive(mine, rz)
            if Y > 1:
                send(mine, mine, sy + 4 * k, ry + 4 * k, to_y_up)
                send(mine, mine, sy + 4 * k + 1, ry + 4 * k + 1, to_y_dn)
            if k == 0:
                yield
        yield
        for k, zi in enumerate(levels):
            if Y > 1:
                arrive(buf.at[core, zi, y_dn], ry + 4 * k)
                send(buf.at[core, zi, y_dn, low], buf.at[core, zi, y_dn, low],
                     sy + 4 * k + 2, ry + 4 * k + 2, to_y_up)
                arrive(buf.at[core, zi, y_up], ry + 4 * k + 1)
                send(buf.at[core, zi, y_up, high], buf.at[core, zi, y_up, high],
                     sy + 4 * k + 3, ry + 4 * k + 3, to_y_dn)
                yield
        for k, zi in enumerate(levels):
            if Y > 1:
                arrive(buf.at[core, zi, y_far, low], ry + 4 * k + 2)
                arrive(buf.at[core, zi, y_far, high], ry + 4 * k + 3)
            if CORE > 1:
                send(buf.at[core, zi], buf.at[core, zi], sc + k, rc + k, to_core)
            yield
        if CORE > 1:
            for k, zi in enumerate(levels):
                arrive(buf.at[1 - core, zi], rc + k)
            yield

    def add(target, value):
        target[...] = (target[...].astype(F32) + value[...].astype(F32)).astype(BF16)

    def scatter_rows(buf, from_core, halves, full, zs, zr, acc):
        sc, rc = sems("send", ZH), sems("recv", ZH)
        sy, ry = sems("send", 4 * ZH), sems("recv", 4 * ZH)
        sz, rz = sems("send", 1), sems("recv", 1)
        levels = [1 - zh, zh][-ZH:]
        if CORE > 1:
            for k, zi in enumerate(levels):
                send(buf.at[1 - core, zi], from_core.at[zi], sc + k, rc + k, to_core)
        yield
        for k, zi in enumerate(levels):
            if CORE > 1:
                arrive(from_core.at[zi], rc + k)
                add(buf.at[core, zi], from_core.at[zi])
            if Y > 1:
                send(buf.at[core, zi, y_far, 0], halves.at[zi, 0], sy + 4 * k, ry + 4 * k, to_y_up)
                send(buf.at[core, zi, y_far, 1], halves.at[zi, 1], sy + 4 * k + 1, ry + 4 * k + 1, to_y_dn)
            yield
        for k, zi in enumerate(levels):
            if Y > 1:
                arrive(halves.at[zi, 0], ry + 4 * k)
                add(buf.at[core, zi, y_up, 0], halves.at[zi, 0])
                send(buf.at[core, zi, y_up], full.at[zi, 0], sy + 4 * k + 2, ry + 4 * k + 2, to_y_up)
                arrive(halves.at[zi, 1], ry + 4 * k + 1)
                add(buf.at[core, zi, y_dn, 1], halves.at[zi, 1])
                send(buf.at[core, zi, y_dn], full.at[zi, 1], sy + 4 * k + 3, ry + 4 * k + 3, to_y_dn)
                yield
        for k, zi in enumerate(levels):
            total = buf[core, zi, y].astype(F32)
            if Y > 1:
                arrive(full.at[zi, 0], ry + 4 * k + 2)
                arrive(full.at[zi, 1], ry + 4 * k + 3)
                total = total + full[zi, 0].astype(F32) + full[zi, 1].astype(F32)
            if ZH > 1 and k == 0:
                zs[...] = total.astype(BF16)
                send(zs, zr, sz, rz, to_zh)
            else:
                acc[...] = total
            yield
        if ZH > 1:
            arrive(zr, rz)
            acc[...] = acc[...] + zr[...].astype(F32)
            yield

    def scatter_cols(buf, halves, full, zs, zu, zd, acc):
        sx, rx = sems("send", 4 * ZL), sems("recv", 4 * ZL)
        sz, ru, rd = sems("send", ZL), sems("recv", ZL), sems("recv", ZL)
        order = []
        for k in range((ZL + 1) // 2):
            order += [ZL - 1 - k, k]
        order = order[:ZL]

        def along(d):
            total = buf[d, x].astype(F32)
            if X > 1:
                arrive(full.at[d, 0], rx + 4 * d + 2)
                arrive(full.at[d, 1], rx + 4 * d + 3)
                total = total + full[d, 0].astype(F32) + full[d, 1].astype(F32)
            acc[d] = total

            def more(source, r):
                arrive(source.at[d], r + d)
                acc[d] = acc[d] + source[d].astype(F32)

            when(both(z < d, z > 0), lambda: more(zu, ru))
            when(both(z > d, z < ZL - 1), lambda: more(zd, rd))

            def store():
                zs[d] = acc[d].astype(BF16)

            when(z != d, store)
            send(zs.at[d], zu.at[d], sz + d, ru + d, to_z_up, z < d)
            send(zs.at[d], zd.at[d], sz + d, rd + d, to_z_dn, z > d)

        if X > 1:
            for d in order:
                send(buf.at[d, x_far, 0], halves.at[d, 0], sx + 4 * d, rx + 4 * d, to_x_up)
                send(buf.at[d, x_far, 1], halves.at[d, 1], sx + 4 * d + 1, rx + 4 * d + 1, to_x_dn)
        yield
        lag = min(3, ZL - 1)
        for k in range(ZL + lag):
            if k < ZL and X > 1:
                d = order[k]
                arrive(halves.at[d, 0], rx + 4 * d)
                add(buf.at[d, x_up, 0], halves.at[d, 0])
                send(buf.at[d, x_up], full.at[d, 0], sx + 4 * d + 2, rx + 4 * d + 2, to_x_up)
                arrive(halves.at[d, 1], rx + 4 * d + 1)
                add(buf.at[d, x_dn, 1], halves.at[d, 1])
                send(buf.at[d, x_dn], full.at[d, 1], sx + 4 * d + 3, rx + 4 * d + 3, to_x_dn)
                yield
            if k >= lag:
                along(order[k - lag])
                yield

        def more(source, r):
            arrive(source.at[z], r + z)
            acc[z] = acc[z] + source[z].astype(F32)

        when(z > 0, lambda: more(zu, ru))
        when(z < ZL - 1, lambda: more(zd, rd))
        yield

    def broadcast_partner():
        owner = col // 2
        core0, y0, zh0 = owner % CORE, (owner // CORE) % Y, owner // (CORE * Y)
        away = (y + Y - y0) % Y
        same_core, same_zh = core == core0, zh == zh0
        chunks = 4
        size = C // chunks
        sz, rz = sems("send", chunks), sems("recv", chunks)
        sy, ry = sems("send", 4 * chunks), sems("recv", 4 * chunks)
        sc, rc = sems("send", chunks), sems("recv", chunks)

        for parity in range(2):
            @pl.when(both(row == owner, col % 2 == parity))
            def _():
                part[...] = gm[:, parity * cols:(parity + 1) * cols, :]

        yield
        source = both(same_core, away == 0)
        for n in range(chunks):
            piece = part.at[pl.ds(n * size, size)]
            if ZH > 1:
                send(piece, piece, sz + n, rz + n, to_zh, both(source, same_zh))
        for n in range(chunks):
            first = part.at[pl.ds(n * size, size // 2)]
            second = part.at[pl.ds(n * size + size // 2, size // 2)]
            piece = part.at[pl.ds(n * size, size)]
            if ZH > 1:
                arrive(piece, rz + n, both(source, jnp.logical_not(same_zh)))
            if Y > 1:
                send(piece, piece, sy + 4 * n, ry + 4 * n, to_y_up, source)
                send(piece, piece, sy + 4 * n + 1, ry + 4 * n + 1, to_y_dn, source)
                yield
                one, three = both(same_core, away == 1), both(same_core, away == 3)
                arrive(piece, ry + 4 * n, one)
                send(first, first, sy + 4 * n + 2, ry + 4 * n + 2, to_y_up, one)
                arrive(piece, ry + 4 * n + 1, three)
                send(second, second, sy + 4 * n + 3, ry + 4 * n + 3, to_y_dn, three)
                yield
                two = both(same_core, away == 2)
                arrive(first, ry + 4 * n + 2, two)
                arrive(second, ry + 4 * n + 3, two)
            if CORE > 1:
                send(piece, piece, sc + n, rc + n, to_core, same_core)
            yield
        if CORE > 1:
            for n in range(chunks):
                piece = part.at[pl.ds(n * size, size)]
                arrive(piece, rc + n, jnp.logical_not(same_core))
            yield

    def place(p):
        return p % CORE, p // (CORE * Y), (p // CORE) % Y

    def spread(block):
        pad = jnp.zeros((LANES - cols, block.shape[1]), block.dtype)
        return jnp.concatenate([block[:cols], pad, block[cols:], pad], axis=0)

    def pair(buf, p, top=0):
        return jnp.concatenate(
            [buf[2 * p, top:top + rows], buf[2 * p + 1, top:top + rows]], axis=1
        )

    def left_terms(side, buf, target):
        turned = side.astype(F32).T.astype(BF16)
        for p in range(R):
            term = jnp.dot(turned, pair(buf, p), preferred_element_type=F32)[:cols].astype(BF16)
            c, h, j = place(p)
            target[c, h, j, 0] = term[:, :LANES]
            target[c, h, j, 1] = term[:, LANES:]

    def turned_block(acc, h):
        turn[0:cols, :] = acc
        return turn[...].T[:cols, :cols]

    g = g_ref[...]
    moment = beta_moment * m_ref[...] + (1.0 - beta_moment) * g.astype(F32)
    mo_ref[...] = moment
    gm[col] = jnp.zeros(gm.shape[1:], BF16)
    lb[col] = jnp.zeros(lb.shape[1:], BF16)
    rb[core, zh, y] = jnp.zeros(rb.shape[3:], BF16)
    gm[col, 0:rows, 0:cols] = g
    gm[col, rows:2 * rows, 0:cols] = moment.astype(BF16)
    lb[col, :, 0:cols] = l_ref[...]
    rb[core, zh, y, :, 0:cols] = r_ref[...]
    turn[...] = jnp.zeros(turn.shape, F32)

    barrier = pltpu.get_barrier_semaphore()

    def greet(device):
        pl.semaphore_signal(barrier, inc=1, device_id=device, device_id_type=MESH)

    always = 0
    for present, devices in (
        (ZH > 1, (to_zh,)), (CORE > 1, (to_core,)), (Y > 1, (to_y_up, to_y_dn)), (X > 1, (to_x_up, to_x_dn)),
    ):
        if present:
            for device in devices:
                greet(device)
                always += 1
    if ZL > 1:
        pl.when(z < ZL - 1)(lambda: greet(to_z_up))
        pl.when(z > 0)(lambda: greet(to_z_dn))
        inner = both(z > 0, z < ZL - 1)
        pl.when(inner)(lambda: pl.semaphore_wait(barrier, always + 2))
        pl.when(jnp.logical_not(inner))(lambda: pl.semaphore_wait(barrier, always + 1))
    else:
        pl.semaphore_wait(barrier, always)

    run(gather_cols(gm), gather_rows(rb))
    rotated = jnp.zeros((2 * rows, LANES), F32)
    for p in range(R):
        both_blocks = jnp.concatenate([gm[2 * p], gm[2 * p + 1]], axis=1)
        rotated = rotated + jnp.dot(both_blocks, spread(rb[place(p)]), preferred_element_type=F32)
    hb[core, zh, y, :, 0:LANES] = rotated[:rows].astype(BF16)
    hb[core, zh, y, :, LANES:2 * LANES] = rotated[rows:].astype(BF16)

    def right_factor_terms():
        left_terms(gm[col, 0:rows, :], gm, gt)
        yield

    run(gather_rows(hb), gather_cols(lb), right_factor_terms())
    rot = jnp.zeros((rows, 2 * LANES), F32)
    for p in range(R):
        rot = rot + jnp.dot(pair(lb, p), spread(hb[place(p)]), preferred_element_type=F32)
    grad_rot, moment_rot = rot[:, 0:cols], rot[:, LANES:LANES + cols]
    second = beta_second * sec_ref[...] + (1.0 - beta_second) * grad_rot * grad_rot
    so_ref[...] = second
    direction = moment_rot / (jnp.sqrt(second) + epsilon)
    facing[...] = jnp.zeros(facing.shape, BF16)
    facing[:, 0:cols] = direction.astype(BF16)

    left_terms(facing[...], lb, bt)
    run(scatter_rows(bt, bt_core, bt_half, bt_full, bt_zs, bt_zr, bt_acc))
    back = jnp.concatenate([bt_acc[0], bt_acc[1]], axis=1).astype(BF16)
    back = jnp.concatenate([back, jnp.zeros((LANES - cols, 2 * LANES), BF16)], axis=0)

    for p in range(R):
        term = jnp.dot(rb[place(p)], back, preferred_element_type=F32).astype(BF16)
        for k in range(2):
            c = 2 * p + k
            for h in range(2):
                ut[c // X, c % X, h] = term[k * cols:(k + 1) * cols, h * LANES:(h + 1) * LANES]
    run(
        scatter_cols(ut, ut_half, ut_full, ut_zs, ut_zu, ut_zd, ut_acc),
        scatter_rows(gt, gt_core, gt_half, gt_full, gt_zs, gt_zr, gt_acc),
        broadcast_partner(),
    )
    left = jnp.zeros((rows, cols), F32)
    for p in range(R):
        left = left + lax.dot_general(
            pair(gm, p), jnp.concatenate([part[2 * p], part[2 * p + 1]], axis=1),
            (((1,), (1,)), ((), ())), preferred_element_type=F32,
        )
    lo_ref[...] = beta_factor * lf_ref[...] + (1.0 - beta_factor) * left
    for h in range(2):
        part_rows = pl.ds(h * cols, cols)
        ro_ref[part_rows, :] = beta_factor * rf_ref[part_rows, :] + (1.0 - beta_factor) * turned_block(gt_acc[h], h)
        up_ref[part_rows, :] = turned_block(ut_acc[z, h], h).astype(BF16)

    for condition, copy in pending:
        when(condition, copy.wait_send)


def per_device(dims, gradient, moment, second, left_factor, right_factor, left_basis_t, right_basis):
    ZH, Y, CORE, ZL, X = dims
    rows, cols = gradient.shape
    C = ZL * X

    def half_blocks(*lead, dtype=BF16):
        return pltpu.VMEM((*lead, 2, cols, LANES), dtype)

    def row_sum():
        return [
            half_blocks(CORE, ZH, Y), half_blocks(ZH, Y), pltpu.VMEM((ZH, 2, cols, LANES), BF16),
            half_blocks(ZH, 2), half_blocks(), half_blocks(), half_blocks(dtype=F32),
        ]

    block = jax.ShapeDtypeStruct((rows, cols), F32)
    return pl.pallas_call(
        functools.partial(kernel, dims),
        out_shape=(block, block, block, block, jax.ShapeDtypeStruct((rows, cols), BF16)),
        in_specs=[pl.BlockSpec(memory_space=pltpu.VMEM)] * 7,
        out_specs=[pl.BlockSpec(memory_space=pltpu.VMEM)] * 5,
        scratch_shapes=[
            pltpu.VMEM((C, 2 * rows, LANES), BF16),
            pltpu.VMEM((C, rows, LANES), BF16),
            pltpu.VMEM((CORE, ZH, Y, rows, LANES), BF16),
            pltpu.VMEM((CORE, ZH, Y, rows, 2 * LANES), BF16),
            *row_sum(),
            *row_sum(),
            half_blocks(ZL, X), pltpu.VMEM((ZL, 2, cols, LANES), BF16), half_blocks(ZL, 2),
            half_blocks(ZL), half_blocks(ZL), half_blocks(ZL), half_blocks(ZL, dtype=F32),
            pltpu.VMEM((C, cols, LANES), BF16),
            pltpu.VMEM((LANES, LANES), F32),
            pltpu.VMEM((rows, LANES), BF16),
            pltpu.SemaphoreType.DMA((256,)),
            pltpu.SemaphoreType.DMA((256,)),
        ],
        compiler_params=pltpu.CompilerParams(
            collective_id=0, has_side_effects=True, vmem_limit_bytes=48 << 20
        ),
    )(gradient, moment, second, left_factor, right_factor, left_basis_t, right_basis)


def build(mesh, dims):
    placed = P("row", "col")
    return jax.shard_map(
        functools.partial(per_device, dims),
        mesh=mesh,
        in_specs=(placed,) * 7,
        out_specs=(placed,) * 5,
        check_vma=False,
    )


def solution(mesh):
    return build(mesh, DIMS)
```

```python
import functools

import jax
import jax.numpy as jnp
from jax import lax
from jax.experimental import pallas as pl
from jax.experimental.pallas import tpu as pltpu
from jax.sharding import PartitionSpec as P

beta_moment = 0.9
beta_second = 0.95
beta_factor = 0.95
epsilon = 1e-08

MESH = pl.DeviceIdType.MESH
LANES = 128
BF16 = jnp.bfloat16
F32 = jnp.float32
DIMS = (2, 4, 2, 8, 4)
LAG = 1
MOMENT_LATER = 0
BASIS_LATER = 0


def run(*steps):
    live = list(steps)
    while live:
        for one in list(live):
            try:
                next(one)
            except StopIteration:
                live.remove(one)


def both(first, second):
    if first is None:
        return second
    if second is None:
        return first
    return jnp.logical_and(first, second)


def when(condition, action):
    if condition is None:
        action()
    else:
        pl.when(condition)(action)


def kernel(
    dims, g_hbm, m_hbm, sec_hbm, lf_hbm, rf_hbm, l_hbm, r_hbm,
    lo_ref, ro_ref, mo_ref, so_ref, up_ref,
    g_ref, m_ref, sec_ref, lf_ref, rf_ref, l_ref, r_ref,
    gb, mb, lb, rb, hg, hm, bt, bt_core, bt_half, bt_full, bt_zs, bt_zr, bt_acc,
    gt, gt_core, gt_half, gt_full, gt_zs, gt_zr, gt_acc,
    ut, ut_half, ut_full, ut_zs, ut_za, ut_zb, ut_zt, ut_zc, ut_other, ut_acc, part, turn, facing,
    ssem, rsem, lsem,
):
    ZH, Y, CORE, ZL, X = dims
    R, C = ZH * Y * CORE, ZL * X
    rows, cols = g_ref.shape
    row, col = lax.axis_index("row"), lax.axis_index("col")
    core, y, zh = row % CORE, (row // CORE) % Y, row // (CORE * Y)
    x, z = col % X, col // X
    H = ZL // 2
    i, ours, there = z % H, z // H * H, (1 - z // H) * H

    def at_row(zh_, y_, core_):
        return ((zh_ * Y + y_) * CORE + core_, col)

    def at_col(z_, x_):
        return (row, z_ * X + x_)

    y_up, y_dn, y_far = (y + 1) % Y, (y + Y - 1) % Y, (y + 2) % Y
    x_up, x_dn, x_far = (x + 1) % X, (x + X - 1) % X, (x + 2) % X
    to_y_up, to_y_dn = at_row(zh, y_up, core), at_row(zh, y_dn, core)
    to_zh, to_core = at_row(1 - zh, y, core), at_row(zh, y, 1 - core)
    to_x_up, to_x_dn = at_col(z, x_up), at_col(z, x_dn)
    mirror = [(col // 2, 2 * row + e) for e in range(2)]
    mirror_core = (col // 2) % CORE
    mirror_y_zh = ((col // 2 // CORE) % Y, col // 2 // (CORE * Y))
    itself = [both(row == col // 2, col % 2 == e) for e in range(2)]
    to_z_up, to_z_dn = at_col(z + 1, x), at_col(z - 1, x)
    some = to_x_up if X > 1 else to_core if CORE > 1 else to_y_up

    counts = {"send": 0, "recv": 0}

    def sems(kind, number):
        first = counts[kind]
        counts[kind] += number
        return first

    pending = []

    def send(source, target, s, r, device, condition=None):
        copy = pltpu.make_async_remote_copy(
            src_ref=source, dst_ref=target, send_sem=ssem.at[s], recv_sem=rsem.at[r],
            device_id=device, device_id_type=MESH,
        )
        when(condition, copy.start)
        pending.append((condition, copy))

    def arrive(target, r, condition=None):
        copy = pltpu.make_async_remote_copy(
            src_ref=target, dst_ref=target, send_sem=ssem.at[0], recv_sem=rsem.at[r],
            device_id=some, device_id_type=MESH,
        )
        when(condition, copy.wait_recv)

    def gather_cols(buf):
        half = buf.shape[1] // 2
        low, high = pl.ds(0, half), pl.ds(half, half)
        sz, rz = sems("send", 2 * ZL), sems("recv", ZL)
        sx, rx = sems("send", 4 * ZL), sems("recv", 4 * ZL)

        def slot(z_, x_):
            return z_ * X + x_

        def items(t):
            if t == 0:
                return [(z, None, 0)]
            return [(z - t, z >= t, 1), (z + t, z + t < ZL, -1)]

        def turn_corner(t):
            if X == 1:
                return
            for zo, ok, _ in items(t):
                arrive(buf.at[slot(zo, x_dn)], rx + 4 * zo, ok)
                send(buf.at[slot(zo, x_dn), low], buf.at[slot(zo, x_dn), low],
                     sx + 4 * zo + 2, rx + 4 * zo + 2, to_x_up, ok)
                arrive(buf.at[slot(zo, x_up)], rx + 4 * zo + 1, ok)
                send(buf.at[slot(zo, x_up), high], buf.at[slot(zo, x_up), high],
                     sx + 4 * zo + 3, rx + 4 * zo + 3, to_x_dn, ok)

        for t in range(ZL):
            for zo, ok, way in items(t):
                here = buf.at[slot(zo, x)]
                if t > 0:
                    arrive(here, rz + zo, ok)
                if way >= 0 and t < ZL - 1:
                    send(here, here, sz + zo, rz + zo, to_z_up, both(ok, z < ZL - 1))
                if way <= 0 and t < ZL - 1:
                    send(here, here, sz + ZL + zo, rz + zo, to_z_dn, both(ok, z > 0))
                if X > 1:
                    send(here, here, sx + 4 * zo, rx + 4 * zo, to_x_up, ok)
                    send(here, here, sx + 4 * zo + 1, rx + 4 * zo + 1, to_x_dn, ok)
            yield
            if t >= LAG:
                turn_corner(t - LAG)
                yield
        for t in range(ZL - LAG, ZL):
            turn_corner(t)
            yield
        if X > 1:
            for zo in range(ZL):
                arrive(buf.at[slot(zo, x_far), low], rx + 4 * zo + 2)
                arrive(buf.at[slot(zo, x_far), high], rx + 4 * zo + 3)
            yield

    def gather_rows(buf):
        half = buf.shape[3] // 2
        low, high = pl.ds(0, half), pl.ds(half, half)
        sz, rz = sems("send", 1), sems("recv", 1)
        sy, ry = sems("send", 4 * ZH), sems("recv", 4 * ZH)
        sc, rc = sems("send", ZH), sems("recv", ZH)
        levels = [zh, 1 - zh][:ZH]
        here = buf.at[core, zh, y]
        if ZH > 1:
            send(here, here, sz, rz, to_zh)
        for k, zi in enumerate(levels):
            mine = buf.at[core, zi, y]
            if k == 1:
                yield
                arrive(mine, rz)
            if Y > 1:
                send(mine, mine, sy + 4 * k, ry + 4 * k, to_y_up)
                send(mine, mine, sy + 4 * k + 1, ry + 4 * k + 1, to_y_dn)
            if k == 0:
                yield
        yield
        for k, zi in enumerate(levels):
            if Y > 1:
                arrive(buf.at[core, zi, y_dn], ry + 4 * k)
                send(buf.at[core, zi, y_dn, low], buf.at[core, zi, y_dn, low],
                     sy + 4 * k + 2, ry + 4 * k + 2, to_y_up)
                arrive(buf.at[core, zi, y_up], ry + 4 * k + 1)
                send(buf.at[core, zi, y_up, high], buf.at[core, zi, y_up, high],
                     sy + 4 * k + 3, ry + 4 * k + 3, to_y_dn)
                yield
        for k, zi in enumerate(levels):
            if Y > 1:
                arrive(buf.at[core, zi, y_far, low], ry + 4 * k + 2)
                arrive(buf.at[core, zi, y_far, high], ry + 4 * k + 3)
            if CORE > 1:
                send(buf.at[core, zi], buf.at[core, zi], sc + k, rc + k, to_core)
            yield
        if CORE > 1:
            for k, zi in enumerate(levels):
                arrive(buf.at[1 - core, zi], rc + k)
            yield

    def add(target, value):
        target[...] = (target[...].astype(F32) + value[...].astype(F32)).astype(BF16)

    def scatter_rows(buf, from_core, halves, full, zs, zr, acc):
        sc, rc = sems("send", ZH), sems("recv", ZH)
        sy, ry = sems("send", 4 * ZH), sems("recv", 4 * ZH)
        sz, rz = sems("send", 1), sems("recv", 1)
        levels = [1 - zh, zh][-ZH:]
        if CORE > 1:
            for k, zi in enumerate(levels):
                send(buf.at[1 - core, zi], from_core.at[zi], sc + k, rc + k, to_core)
        yield
        for k, zi in enumerate(levels):
            if CORE > 1:
                arrive(from_core.at[zi], rc + k)
                add(buf.at[core, zi], from_core.at[zi])
            if Y > 1:
                send(buf.at[core, zi, y_far, 0], halves.at[zi, 0], sy + 4 * k, ry + 4 * k, to_y_up)
                send(buf.at[core, zi, y_far, 1], halves.at[zi, 1], sy + 4 * k + 1, ry + 4 * k + 1, to_y_dn)
            yield
        for k, zi in enumerate(levels):
            if Y > 1:
                arrive(halves.at[zi, 0], ry + 4 * k)
                add(buf.at[core, zi, y_up, 0], halves.at[zi, 0])
                send(buf.at[core, zi, y_up], full.at[zi, 0], sy + 4 * k + 2, ry + 4 * k + 2, to_y_up)
                arrive(halves.at[zi, 1], ry + 4 * k + 1)
                add(buf.at[core, zi, y_dn, 1], halves.at[zi, 1])
                send(buf.at[core, zi, y_dn], full.at[zi, 1], sy + 4 * k + 3, ry + 4 * k + 3, to_y_dn)
                yield
        for k, zi in enumerate(levels):
            total = buf[core, zi, y].astype(F32)
            if Y > 1:
                arrive(full.at[zi, 0], ry + 4 * k + 2)
                arrive(full.at[zi, 1], ry + 4 * k + 3)
                total = total + full[zi, 0].astype(F32) + full[zi, 1].astype(F32)
            if ZH > 1 and k == 0:
                zs[...] = total.astype(BF16)
                send(zs, zr, sz, rz, to_zh)
            else:
                acc[...] = total
            yield
        if ZH > 1:
            arrive(zr, rz)
            acc[...] = acc[...] + zr[...].astype(F32)
            yield

    def scatter_cols(buf, halves, full, zs, za, zb, zt, zc, other, acc):
        sx, rx = sems("send", 4 * ZL), sems("recv", 4 * ZL)
        sz, ra, rb_ = sems("send", ZL), sems("recv", H), sems("recv", H)
        sc, rc = sems("send", 1), sems("recv", 1)
        order = [there + j for j in range(H)] + [ours + j for j in range(H)]
        if X > 1:
            for k, d in enumerate(order):
                send(buf.at[d, x_far, 0], halves.at[k, 0], sx + 4 * k, rx + 4 * k, to_x_up)
                send(buf.at[d, x_far, 1], halves.at[k, 1], sx + 4 * k + 1, rx + 4 * k + 1, to_x_dn)
        yield

        def along(k):
            d, j = order[k], k % H
            total = buf[d, x].astype(F32)
            if X > 1:
                arrive(full.at[k, 0], rx + 4 * k + 2)
                arrive(full.at[k, 1], rx + 4 * k + 3)
                total = total + full[k, 0].astype(F32) + full[k, 1].astype(F32)
            zs[k] = total.astype(BF16)
            target, keep, r = (za, other, ra) if k < H else (zb, acc, rb_)
            send(zs.at[k], target.at[i], sz + k, r + i, at_col(ours + j, x), i != j)

            @pl.when(i == j)
            def _():
                keep[...] = total

        def gathered(source, r, into):
            for j in range(H):
                @pl.when(i != j)
                def _():
                    arrive(source.at[j], r + j)
                    into[...] = into[...] + source[j].astype(F32)

        lag = min(2, ZL - 1)
        for k in range(ZL + lag):
            if k < ZL and X > 1:
                d = order[k]
                arrive(halves.at[k, 0], rx + 4 * k)
                add(buf.at[d, x_up, 0], halves.at[k, 0])
                send(buf.at[d, x_up], full.at[k, 0], sx + 4 * k + 2, rx + 4 * k + 2, to_x_up)
                arrive(halves.at[k, 1], rx + 4 * k + 1)
                add(buf.at[d, x_dn, 1], halves.at[k, 1])
                send(buf.at[d, x_dn], full.at[k, 1], sx + 4 * k + 3, rx + 4 * k + 3, to_x_dn)
                yield
            if k >= lag:
                along(k - lag)
                yield
            if k - lag == min(H + 1, ZL - 1):
                gathered(za, ra, other)
                zt[...] = other[...].astype(BF16)
                send(zt, zc, sc, rc, at_col(there + i, x))
                yield
        gathered(zb, rb_, acc)
        arrive(zc, rc)
        acc[...] = acc[...] + zc[...].astype(F32)
        yield

    def exchange():
        sx, rx = sems("send", 2), sems("recv", 2)
        own_place = part.at[core, zh, y]
        for e in range(2):
            send(gb.at[col, pl.ds(e * cols, cols)], part.at[mirror_core, mirror_y_zh[1], mirror_y_zh[0], col % 2],
                 sx + e, rx + col % 2, mirror[e], jnp.logical_not(itself[e]))

            @pl.when(itself[e])
            def _():
                part[core, zh, y, e] = gb[col, e * cols:(e + 1) * cols, :]

        yield
        for e in range(2):
            arrive(own_place.at[e], rx + e, jnp.logical_not(itself[e]))

    def place(p):
        return p % CORE, p // (CORE * Y), (p // CORE) % Y

    def spread(block):
        pad = jnp.zeros((LANES - cols, block.shape[1]), block.dtype)
        return jnp.concatenate([block[:cols], pad, block[cols:], pad], axis=0)

    def pair(buf, p):
        return jnp.concatenate([buf[2 * p], buf[2 * p + 1]], axis=1)

    def left_terms(side, buf, target):
        turned = side.astype(F32).T.astype(BF16)
        for p in range(R):
            term = jnp.dot(turned, pair(buf, p), preferred_element_type=F32)[:cols].astype(BF16)
            c, h, j = place(p)
            target[c, h, j, 0] = term[:, :LANES]
            target[c, h, j, 1] = term[:, LANES:]

    def turned_block(acc):
        turn[0:cols, :] = acc
        return turn[...].T[:cols, :cols]

    loads = [
        pltpu.make_async_copy(source, target, lsem.at[n])
        for n, (source, target) in enumerate((
            (g_hbm, g_ref), (m_hbm, m_ref), (r_hbm, r_ref), (l_hbm, l_ref),
            (sec_hbm, sec_ref), (lf_hbm, lf_ref), (rf_hbm, rf_ref),
        ))
    ]
    for load in loads:
        load.start()

    barrier = pltpu.get_barrier_semaphore()

    def greet(device):
        pl.semaphore_signal(barrier, inc=1, device_id=device, device_id_type=MESH)

    greeted = 0
    for present, devices in (
        (ZH > 1, (to_zh,)), (CORE > 1, (to_core,)), (Y > 1, (to_y_up, to_y_dn)), (X > 1, (to_x_up, to_x_dn)),
        (True, (at_col(there + i, x),)),
    ):
        if present:
            for device in devices:
                greet(device)
                greeted += 1
    for j in range(H):
        pl.when(i != j)(functools.partial(greet, at_col(ours + j, x)))
    greeted += H - 1
    edge = jnp.logical_or(z == H - 1, z == H)
    if H > 1:
        pl.when(z == H - 1)(lambda: greet(to_z_up))
        pl.when(z == H)(lambda: greet(to_z_dn))

    for e in range(2):
        pl.when(jnp.logical_not(itself[e]))(functools.partial(greet, mirror[e]))
    expected = greeted + jnp.where(row == col // 2, 1, 2)
    if H > 1:
        expected = expected + jnp.where(edge, 1, 0)

    gb[col] = jnp.zeros(gb.shape[1:], BF16)
    mb[col] = jnp.zeros(mb.shape[1:], BF16)
    lb[col] = jnp.zeros(lb.shape[1:], BF16)
    rb[core, zh, y] = jnp.zeros(rb.shape[3:], BF16)
    facing[...] = jnp.zeros(facing.shape, BF16)
    turn[...] = jnp.zeros(turn.shape, F32)
    for load in loads[:4]:
        load.wait()
    g = g_ref[...]
    moment = beta_moment * m_ref[...] + (1.0 - beta_moment) * g.astype(F32)
    mo_ref[...] = moment
    gb[col, :, 0:cols] = g
    mb[col, :, 0:cols] = moment.astype(BF16)
    lb[col, :, 0:cols] = l_ref[...]
    rb[core, zh, y, :, 0:cols] = r_ref[...]

    pl.semaphore_wait(barrier, expected)

    def rotate(source, target):
        rotated = jnp.zeros((rows, LANES), F32)
        for p in range(R):
            rotated = rotated + jnp.dot(pair(source, p), spread(rb[place(p)]), preferred_element_type=F32)
        target[core, zh, y] = rotated.astype(BF16)

    ready = []

    def gradient_steps():
        yield from gather_cols(gb)
        while not ready:
            yield
        rotate(gb, hg)
        yield from gather_rows(hg)

    factor = scatter_rows(gt, gt_core, gt_half, gt_full, gt_zs, gt_zr, gt_acc)

    def moment_steps():
        for _ in range(MOMENT_LATER):
            yield
        yield from gather_cols(mb)
        rotate(mb, hm)
        rest = gather_rows(hm)
        next(rest)
        left_terms(gb[col], gb, gt)
        next(factor)
        yield from rest

    def basis_steps():
        for _ in range(BASIS_LATER):
            yield
        yield from gather_cols(lb)

    def other_steps():
        swap = exchange()
        next(swap)
        yield from gather_rows(rb)
        ready.append(True)
        yield from swap
        yield from gather_rows(part)

    run(gradient_steps(), moment_steps(), basis_steps(), other_steps())
    for load in loads[4:]:
        load.wait()
    rot = jnp.zeros((rows, 2 * LANES), F32)
    for p in range(R):
        both_rotated = jnp.concatenate([spread(hg[place(p)]), spread(hm[place(p)])], axis=1)
        rot = rot + jnp.dot(pair(lb, p), both_rotated, preferred_element_type=F32)
    grad_rot, moment_rot = rot[:, 0:cols], rot[:, LANES:LANES + cols]
    second = beta_second * sec_ref[...] + (1.0 - beta_second) * grad_rot * grad_rot
    so_ref[...] = second
    direction = moment_rot / (jnp.sqrt(second) + epsilon)
    facing[:, 0:cols] = direction.astype(BF16)

    left_terms(facing[...], lb, bt)
    main = scatter_rows(bt, bt_core, bt_half, bt_full, bt_zs, bt_zr, bt_acc)
    next(main)
    next(factor)
    next(factor)
    run(main)
    next(factor, None)
    next(factor, None)
    back = jnp.concatenate([bt_acc[0], bt_acc[1]], axis=1).astype(BF16)
    back = jnp.concatenate([back, jnp.zeros((LANES - cols, 2 * LANES), BF16)], axis=0)

    for p in range(R):
        term = jnp.dot(rb[place(p)], back, preferred_element_type=F32).astype(BF16)
        for k in range(2):
            c = 2 * p + k
            for h in range(2):
                ut[c // X, c % X, h] = term[k * cols:(k + 1) * cols, h * LANES:(h + 1) * LANES]
    main = scatter_cols(ut, ut_half, ut_full, ut_zs, ut_za, ut_zb, ut_zt, ut_zc, ut_other, ut_acc)
    for k in range(8):
        next(main, None)
        if k % 2 == 1:
            next(factor, None)
    run(factor)
    left = jnp.zeros((rows, cols), F32)
    for p in range(R):
        left = left + lax.dot_general(
            pair(gb, p), jnp.concatenate([part[place(p)][0], part[place(p)][1]], axis=1),
            (((1,), (1,)), ((), ())), preferred_element_type=F32,
        )
    lo_ref[...] = beta_factor * lf_ref[...] + (1.0 - beta_factor) * left
    for h in range(2):
        half_rows = pl.ds(h * cols, cols)
        ro_ref[half_rows, :] = beta_factor * rf_ref[half_rows, :] + (1.0 - beta_factor) * turned_block(gt_acc[h])
    run(main)
    for h in range(2):
        up_ref[pl.ds(h * cols, cols), :] = turned_block(ut_acc[h]).astype(BF16)

    for condition, copy in pending:
        when(condition, copy.wait_send)


def per_device(dims, gradient, moment, second, left_factor, right_factor, left_basis_t, right_basis):
    ZH, Y, CORE, ZL, X = dims
    rows, cols = gradient.shape
    C = ZL * X

    def half_blocks(*lead, dtype=BF16):
        return pltpu.VMEM((*lead, 2, cols, LANES), dtype)

    def row_sum():
        return [
            half_blocks(CORE, ZH, Y), half_blocks(ZH, Y), pltpu.VMEM((ZH, 2, cols, LANES), BF16),
            half_blocks(ZH, 2), half_blocks(), half_blocks(), half_blocks(dtype=F32),
        ]

    block = jax.ShapeDtypeStruct((rows, cols), F32)
    return pl.pallas_call(
        functools.partial(kernel, dims),
        out_shape=(block, block, block, block, jax.ShapeDtypeStruct((rows, cols), BF16)),
        in_specs=[pl.BlockSpec(memory_space=pl.ANY)] * 7,
        out_specs=[pl.BlockSpec(memory_space=pltpu.VMEM)] * 5,
        scratch_shapes=[
            *(pltpu.VMEM((rows, cols), dtype) for dtype in (BF16, F32, F32, F32, F32, BF16, BF16)),
            *(pltpu.VMEM((C, rows, LANES), BF16) for _ in range(3)),
            *(pltpu.VMEM((CORE, ZH, Y, rows, LANES), BF16) for _ in range(3)),
            *row_sum(),
            *row_sum(),
            half_blocks(ZL, X), pltpu.VMEM((ZL, 2, cols, LANES), BF16), half_blocks(ZL, 2),
            half_blocks(ZL), half_blocks(ZL // 2), half_blocks(ZL // 2), half_blocks(), half_blocks(),
            half_blocks(dtype=F32), half_blocks(dtype=F32),
            half_blocks(CORE, ZH, Y),
            pltpu.VMEM((LANES, LANES), F32),
            pltpu.VMEM((rows, LANES), BF16),
            pltpu.SemaphoreType.DMA((320,)),
            pltpu.SemaphoreType.DMA((320,)),
            pltpu.SemaphoreType.DMA((7,)),
        ],
        compiler_params=pltpu.CompilerParams(
            collective_id=0, has_side_effects=True, vmem_limit_bytes=48 << 20
        ),
    )(gradient, moment, second, left_factor, right_factor, left_basis_t, right_basis)


def build(mesh, dims):
    placed = P("row", "col")
    return jax.shard_map(
        functools.partial(per_device, dims),
        mesh=mesh,
        in_specs=(placed,) * 7,
        out_specs=(placed,) * 5,
        check_vma=False,
    )


def solution(mesh):
    return build(mesh, DIMS)
```

```python
import functools

import jax
import jax.numpy as jnp
from jax import lax
from jax.experimental import pallas as pl
from jax.experimental.pallas import tpu as pltpu
from jax.sharding import PartitionSpec as P

beta_moment = 0.9
beta_second = 0.95
beta_factor = 0.95
epsilon = 1e-08

MESH = pl.DeviceIdType.MESH
LANES = 128
BF16 = jnp.bfloat16
F32 = jnp.float32
DIMS = (2, 4, 2, 8, 4)
LAG = 2
LEFT_FROM = 0
LEFT_EVERY = 2
FACTOR_AT = {0: 1, 4: 1, 10: 1}
PARTNER_AT = {0: 2, 4: 1, 5: 1, 8: 1, 9: 1, 12: 1}
RIGHT_AT = {3: 1, 9: 2, 11: 1, 12: 1, 13: 2}


def run(*steps):
    live = list(steps)
    while live:
        for one in list(live):
            try:
                next(one)
            except StopIteration:
                live.remove(one)


def both(first, second):
    if first is None:
        return second
    if second is None:
        return first
    return jnp.logical_and(first, second)


def when(condition, action):
    if condition is None:
        action()
    else:
        pl.when(condition)(action)


def kernel(
    dims, g_hbm, m_hbm, sec_hbm, lf_hbm, rf_hbm, l_hbm, r_hbm,
    lo_ref, ro_ref, mo_ref, so_ref, up_ref,
    g_ref, m_ref, sec_ref, lf_ref, rf_ref, l_ref, r_ref,
    gb, mb, lb, rb, hg, hm, bt, bt_core, bt_half, bt_full, bt_zs, bt_zr, bt_acc,
    gt, gt_core, gt_half, gt_full, gt_zs, gt_zr, gt_acc,
    ut, ut_half, ut_full, ut_zs, ut_za, ut_zb, ut_zt, ut_zc, ut_other, ut_acc, part, turn, facing,
    ssem, rsem, lsem,
):
    ZH, Y, CORE, ZL, X = dims
    R, C = ZH * Y * CORE, ZL * X
    rows, cols = g_ref.shape
    row, col = lax.axis_index("row"), lax.axis_index("col")
    core, y, zh = row % CORE, (row // CORE) % Y, row // (CORE * Y)
    x, z = col % X, col // X
    H = ZL // 2
    i, ours, there = z % H, z // H * H, (1 - z // H) * H

    def at_row(zh_, y_, core_):
        return ((zh_ * Y + y_) * CORE + core_, col)

    def at_col(z_, x_):
        return (row, z_ * X + x_)

    y_up, y_dn, y_far = (y + 1) % Y, (y + Y - 1) % Y, (y + 2) % Y
    x_up, x_dn, x_far = (x + 1) % X, (x + X - 1) % X, (x + 2) % X
    to_y_up, to_y_dn = at_row(zh, y_up, core), at_row(zh, y_dn, core)
    to_zh, to_core = at_row(1 - zh, y, core), at_row(zh, y, 1 - core)
    to_x_up, to_x_dn = at_col(z, x_up), at_col(z, x_dn)
    mirror = [(col // 2, 2 * row + e) for e in range(2)]
    mirror_core = (col // 2) % CORE
    mirror_y_zh = ((col // 2 // CORE) % Y, col // 2 // (CORE * Y))
    itself = [both(row == col // 2, col % 2 == e) for e in range(2)]
    to_z_up, to_z_dn = at_col(z + 1, x), at_col(z - 1, x)
    some = to_x_up if X > 1 else to_core if CORE > 1 else to_y_up

    counts = {"send": 0, "recv": 0}

    def sems(kind, number):
        first = counts[kind]
        counts[kind] += number
        return first

    pending = []

    def send(source, target, s, r, device, condition=None):
        copy = pltpu.make_async_remote_copy(
            src_ref=source, dst_ref=target, send_sem=ssem.at[s], recv_sem=rsem.at[r],
            device_id=device, device_id_type=MESH,
        )
        when(condition, copy.start)
        pending.append((condition, copy))

    def arrive(target, r, condition=None):
        copy = pltpu.make_async_remote_copy(
            src_ref=target, dst_ref=target, send_sem=ssem.at[0], recv_sem=rsem.at[r],
            device_id=some, device_id_type=MESH,
        )
        when(condition, copy.wait_recv)

    def gather_cols(buf):
        half = buf.shape[1] // 2
        low, high = pl.ds(0, half), pl.ds(half, half)
        lag = min(LAG, ZL)
        sz, rz = sems("send", 2 * ZL), sems("recv", ZL)
        sx, rx = sems("send", 4 * ZL), sems("recv", 4 * ZL)

        def slot(z_, x_):
            return z_ * X + x_

        def items(t):
            if t == 0:
                return [(z, None, 0)]
            return [(z - t, z >= t, 1), (z + t, z + t < ZL, -1)]

        def turn_corner(t):
            if X == 1:
                return
            for zo, ok, _ in items(t):
                arrive(buf.at[slot(zo, x_dn)], rx + 4 * zo, ok)
                send(buf.at[slot(zo, x_dn), low], buf.at[slot(zo, x_dn), low],
                     sx + 4 * zo + 2, rx + 4 * zo + 2, to_x_up, ok)
                arrive(buf.at[slot(zo, x_up)], rx + 4 * zo + 1, ok)
                send(buf.at[slot(zo, x_up), high], buf.at[slot(zo, x_up), high],
                     sx + 4 * zo + 3, rx + 4 * zo + 3, to_x_dn, ok)

        for t in range(ZL):
            for zo, ok, way in items(t):
                here = buf.at[slot(zo, x)]
                if t > 0:
                    arrive(here, rz + zo, ok)
                if way >= 0 and t < ZL - 1:
                    send(here, here, sz + zo, rz + zo, to_z_up, both(ok, z < ZL - 1))
                if way <= 0 and t < ZL - 1:
                    send(here, here, sz + ZL + zo, rz + zo, to_z_dn, both(ok, z > 0))
                if X > 1:
                    send(here, here, sx + 4 * zo, rx + 4 * zo, to_x_up, ok)
                    send(here, here, sx + 4 * zo + 1, rx + 4 * zo + 1, to_x_dn, ok)
            yield
            if t >= lag:
                turn_corner(t - lag)
                yield
        for t in range(ZL - lag, ZL):
            turn_corner(t)
            yield
        if X > 1:
            for zo in range(ZL):
                arrive(buf.at[slot(zo, x_far), low], rx + 4 * zo + 2)
                arrive(buf.at[slot(zo, x_far), high], rx + 4 * zo + 3)
            yield

    def gather_z(buf):
        sz, rz = sems("send", 2 * ZL), sems("recv", ZL)
        for t in range(ZL):
            ways = [(z, None, 0)] if t == 0 else [(z - t, z >= t, 1), (z + t, z + t < ZL, -1)]
            for zo, ok, way in ways:
                here = buf.at[zo * X + x]
                if t > 0:
                    arrive(here, rz + zo, ok)
                if way >= 0 and t < ZL - 1:
                    send(here, here, sz + zo, rz + zo, to_z_up, both(ok, z < ZL - 1))
                if way <= 0 and t < ZL - 1:
                    send(here, here, sz + ZL + zo, rz + zo, to_z_dn, both(ok, z > 0))
            yield

    def gather_x(buf):
        if X == 1:
            return
        half = buf.shape[1] // 2
        low, high = pl.ds(0, half), pl.ds(half, half)
        sx, rx = sems("send", 4 * ZL), sems("recv", 4 * ZL)
        for zo in range(ZL):
            here = buf.at[zo * X + x]
            send(here, here, sx + 4 * zo, rx + 4 * zo, to_x_up)
            send(here, here, sx + 4 * zo + 1, rx + 4 * zo + 1, to_x_dn)
        yield
        for zo in range(ZL):
            below, above = buf.at[zo * X + x_dn], buf.at[zo * X + x_up]
            arrive(below, rx + 4 * zo)
            send(below.at[low], below.at[low], sx + 4 * zo + 2, rx + 4 * zo + 2, to_x_up)
            arrive(above, rx + 4 * zo + 1)
            send(above.at[high], above.at[high], sx + 4 * zo + 3, rx + 4 * zo + 3, to_x_dn)
            if zo % 2 == 1:
                yield
        for zo in range(ZL):
            far = buf.at[zo * X + x_far]
            arrive(far.at[low], rx + 4 * zo + 2)
            arrive(far.at[high], rx + 4 * zo + 3)
        yield

    def gather_rows(buf):
        half = buf.shape[3] // 2
        low, high = pl.ds(0, half), pl.ds(half, half)
        sz, rz = sems("send", 1), sems("recv", 1)
        sy, ry = sems("send", 4 * ZH), sems("recv", 4 * ZH)
        sc, rc = sems("send", ZH), sems("recv", ZH)
        levels = [zh, 1 - zh][:ZH]
        here = buf.at[core, zh, y]
        if ZH > 1:
            send(here, here, sz, rz, to_zh)
        for k, zi in enumerate(levels):
            mine = buf.at[core, zi, y]
            if k == 1:
                yield
                arrive(mine, rz)
            if Y > 1:
                send(mine, mine, sy + 4 * k, ry + 4 * k, to_y_up)
                send(mine, mine, sy + 4 * k + 1, ry + 4 * k + 1, to_y_dn)
            if k == 0:
                yield
        yield
        for k, zi in enumerate(levels):
            if Y > 1:
                arrive(buf.at[core, zi, y_dn], ry + 4 * k)
                send(buf.at[core, zi, y_dn, low], buf.at[core, zi, y_dn, low],
                     sy + 4 * k + 2, ry + 4 * k + 2, to_y_up)
                arrive(buf.at[core, zi, y_up], ry + 4 * k + 1)
                send(buf.at[core, zi, y_up, high], buf.at[core, zi, y_up, high],
                     sy + 4 * k + 3, ry + 4 * k + 3, to_y_dn)
                yield
        for k, zi in enumerate(levels):
            if Y > 1:
                arrive(buf.at[core, zi, y_far, low], ry + 4 * k + 2)
                arrive(buf.at[core, zi, y_far, high], ry + 4 * k + 3)
            if CORE > 1:
                send(buf.at[core, zi], buf.at[core, zi], sc + k, rc + k, to_core)
            yield
        if CORE > 1:
            for k, zi in enumerate(levels):
                arrive(buf.at[1 - core, zi], rc + k)
            yield

    def add(target, value):
        target[...] = (target[...].astype(F32) + value[...].astype(F32)).astype(BF16)

    def scatter_rows(buf, from_core, halves, full, zs, zr, acc):
        sc, rc = sems("send", ZH), sems("recv", ZH)
        sy, ry = sems("send", 4 * ZH), sems("recv", 4 * ZH)
        sz, rz = sems("send", 1), sems("recv", 1)
        levels = [1 - zh, zh][-ZH:]
        if CORE > 1:
            for k, zi in enumerate(levels):
                send(buf.at[1 - core, zi], from_core.at[zi], sc + k, rc + k, to_core)
        yield
        for k, zi in enumerate(levels):
            if CORE > 1:
                arrive(from_core.at[zi], rc + k)
                add(buf.at[core, zi], from_core.at[zi])
            if Y > 1:
                send(buf.at[core, zi, y_far, 0], halves.at[zi, 0], sy + 4 * k, ry + 4 * k, to_y_up)
                send(buf.at[core, zi, y_far, 1], halves.at[zi, 1], sy + 4 * k + 1, ry + 4 * k + 1, to_y_dn)
            yield
        for k, zi in enumerate(levels):
            if Y > 1:
                arrive(halves.at[zi, 0], ry + 4 * k)
                add(buf.at[core, zi, y_up, 0], halves.at[zi, 0])
                send(buf.at[core, zi, y_up], full.at[zi, 0], sy + 4 * k + 2, ry + 4 * k + 2, to_y_up)
                arrive(halves.at[zi, 1], ry + 4 * k + 1)
                add(buf.at[core, zi, y_dn, 1], halves.at[zi, 1])
                send(buf.at[core, zi, y_dn], full.at[zi, 1], sy + 4 * k + 3, ry + 4 * k + 3, to_y_dn)
                yield
        for k, zi in enumerate(levels):
            total = buf[core, zi, y].astype(F32)
            if Y > 1:
                arrive(full.at[zi, 0], ry + 4 * k + 2)
                arrive(full.at[zi, 1], ry + 4 * k + 3)
                total = total + full[zi, 0].astype(F32) + full[zi, 1].astype(F32)
            if ZH > 1 and k == 0:
                zs[...] = total.astype(BF16)
                send(zs, zr, sz, rz, to_zh)
            else:
                acc[...] = total
            yield
        if ZH > 1:
            arrive(zr, rz)
            acc[...] = acc[...] + zr[...].astype(F32)
            yield

    def scatter_cols(buf, halves, full, zs, za, zb, zt, zc, other, acc):
        sx, rx = sems("send", 4 * ZL), sems("recv", 4 * ZL)
        sz, ra, rb_ = sems("send", ZL), sems("recv", H), sems("recv", H)
        sc, rc = sems("send", 1), sems("recv", 1)
        order = [there + j for j in range(H)] + [ours + j for j in range(H)]
        if X > 1:
            for k, d in enumerate(order):
                send(buf.at[d, x_far, 0], halves.at[k, 0], sx + 4 * k, rx + 4 * k, to_x_up)
                send(buf.at[d, x_far, 1], halves.at[k, 1], sx + 4 * k + 1, rx + 4 * k + 1, to_x_dn)
        yield

        def along(k):
            d, j = order[k], k % H
            total = buf[d, x].astype(F32)
            if X > 1:
                arrive(full.at[k, 0], rx + 4 * k + 2)
                arrive(full.at[k, 1], rx + 4 * k + 3)
                total = total + full[k, 0].astype(F32) + full[k, 1].astype(F32)
            zs[k] = total.astype(BF16)
            target, keep, r = (za, other, ra) if k < H else (zb, acc, rb_)
            send(zs.at[k], target.at[i], sz + k, r + i, at_col(ours + j, x), i != j)

            @pl.when(i == j)
            def _():
                keep[...] = total

        def gathered(source, r, into):
            for j in range(H):
                @pl.when(i != j)
                def _():
                    arrive(source.at[j], r + j)
                    into[...] = into[...] + source[j].astype(F32)

        lag = min(2, ZL - 1)
        for k in range(ZL + lag):
            if k < ZL and X > 1:
                d = order[k]
                arrive(halves.at[k, 0], rx + 4 * k)
                add(buf.at[d, x_up, 0], halves.at[k, 0])
                send(buf.at[d, x_up], full.at[k, 0], sx + 4 * k + 2, rx + 4 * k + 2, to_x_up)
                arrive(halves.at[k, 1], rx + 4 * k + 1)
                add(buf.at[d, x_dn, 1], halves.at[k, 1])
                send(buf.at[d, x_dn], full.at[k, 1], sx + 4 * k + 3, rx + 4 * k + 3, to_x_dn)
                yield
            if k >= lag:
                along(k - lag)
                yield
            if k - lag == min(H + 1, ZL - 1):
                gathered(za, ra, other)
                zt[...] = other[...].astype(BF16)
                send(zt, zc, sc, rc, at_col(there + i, x))
                yield
        gathered(zb, rb_, acc)
        arrive(zc, rc)
        acc[...] = acc[...] + zc[...].astype(F32)
        yield

    def exchange():
        sx, rx = sems("send", 2), sems("recv", 2)
        own_place = part.at[core, zh, y]
        for e in range(2):
            send(gb.at[col, pl.ds(e * cols, cols)], part.at[mirror_core, mirror_y_zh[1], mirror_y_zh[0], col % 2],
                 sx + e, rx + col % 2, mirror[e], jnp.logical_not(itself[e]))

            @pl.when(itself[e])
            def _():
                part[core, zh, y, e] = gb[col, e * cols:(e + 1) * cols, :]

        yield
        for e in range(2):
            arrive(own_place.at[e], rx + e, jnp.logical_not(itself[e]))

    def place(p):
        return p % CORE, p // (CORE * Y), (p // CORE) % Y

    def spread(block):
        pad = jnp.zeros((LANES - cols, block.shape[1]), block.dtype)
        return jnp.concatenate([block[:cols], pad, block[cols:], pad], axis=0)

    def pair(buf, p):
        return jnp.concatenate([buf[2 * p], buf[2 * p + 1]], axis=1)

    def left_terms(side, buf, target):
        turned = side.astype(F32).T.astype(BF16)
        for p in range(R):
            term = jnp.dot(turned, pair(buf, p), preferred_element_type=F32)[:cols].astype(BF16)
            c, h, j = place(p)
            target[c, h, j, 0] = term[:, :LANES]
            target[c, h, j, 1] = term[:, LANES:]

    def turned_block(acc):
        turn[0:cols, :] = acc
        return turn[...].T[:cols, :cols]

    loads = [
        pltpu.make_async_copy(source, target, lsem.at[n])
        for n, (source, target) in enumerate((
            (g_hbm, g_ref), (m_hbm, m_ref), (r_hbm, r_ref), (l_hbm, l_ref),
            (sec_hbm, sec_ref), (lf_hbm, lf_ref), (rf_hbm, rf_ref),
        ))
    ]
    for load in loads:
        load.start()

    barrier = pltpu.get_barrier_semaphore()

    def greet(device):
        pl.semaphore_signal(barrier, inc=1, device_id=device, device_id_type=MESH)

    greeted = 0
    for present, devices in (
        (ZH > 1, (to_zh,)), (CORE > 1, (to_core,)), (Y > 1, (to_y_up, to_y_dn)), (X > 1, (to_x_up, to_x_dn)),
        (True, (at_col(there + i, x),)),
    ):
        if present:
            for device in devices:
                greet(device)
                greeted += 1
    for j in range(H):
        pl.when(i != j)(functools.partial(greet, at_col(ours + j, x)))
    greeted += H - 1
    edge = jnp.logical_or(z == H - 1, z == H)
    if H > 1:
        pl.when(z == H - 1)(lambda: greet(to_z_up))
        pl.when(z == H)(lambda: greet(to_z_dn))

    for e in range(2):
        pl.when(jnp.logical_not(itself[e]))(functools.partial(greet, mirror[e]))
    expected = greeted + jnp.where(row == col // 2, 1, 2)
    if H > 1:
        expected = expected + jnp.where(edge, 1, 0)

    gb[col] = jnp.zeros(gb.shape[1:], BF16)
    mb[col] = jnp.zeros(mb.shape[1:], BF16)
    lb[col] = jnp.zeros(lb.shape[1:], BF16)
    rb[core, zh, y] = jnp.zeros(rb.shape[3:], BF16)
    facing[...] = jnp.zeros(facing.shape, BF16)
    turn[...] = jnp.zeros(turn.shape, F32)
    for load in loads[:4]:
        load.wait()
    g = g_ref[...]
    moment = beta_moment * m_ref[...] + (1.0 - beta_moment) * g.astype(F32)
    mo_ref[...] = moment
    gb[col, :, 0:cols] = g
    mb[col, :, 0:cols] = moment.astype(BF16)
    lb[col, :, 0:cols] = l_ref[...]
    rb[core, zh, y, :, 0:cols] = r_ref[...]

    pl.semaphore_wait(barrier, expected)

    def rotate(source, target):
        rotated = jnp.zeros((rows, LANES), F32)
        for p in range(R):
            rotated = rotated + jnp.dot(pair(source, p), spread(rb[place(p)]), preferred_element_type=F32)
        target[core, zh, y] = rotated.astype(BF16)

    factor = scatter_rows(gt, gt_core, gt_half, gt_full, gt_zs, gt_zr, gt_acc)
    swap, partner = exchange(), gather_rows(part)
    left_z, left_x = gather_z(lb), gather_x(lb)
    grad_cols, moment_cols, right_rows = gather_cols(gb), gather_cols(mb), gather_rows(rb)
    for k in range(14):
        next(grad_cols, None)
        next(moment_cols, None)
        for _ in range(RIGHT_AT.get(k, 0)):
            next(right_rows, None)
        if k >= LEFT_FROM and (k - LEFT_FROM) % LEFT_EVERY == 0:
            next(left_z, None)
    run(grad_cols, moment_cols, right_rows)
    rotate(gb, hg)
    grad_rows, moment_rows = gather_rows(hg), gather_rows(hm)
    next(grad_rows)
    rotate(mb, hm)
    next(moment_rows)
    run(left_z)
    next(left_x, None)
    next(swap)
    left_terms(gb[col], gb, gt)
    next(factor)
    run(grad_rows, moment_rows, left_x)
    next(factor)
    next(factor)
    for load in loads[4:]:
        load.wait()
    rot = jnp.zeros((rows, 2 * LANES), F32)
    for p in range(R):
        both_rotated = jnp.concatenate([spread(hg[place(p)]), spread(hm[place(p)])], axis=1)
        rot = rot + jnp.dot(pair(lb, p), both_rotated, preferred_element_type=F32)
    grad_rot, moment_rot = rot[:, 0:cols], rot[:, LANES:LANES + cols]
    second = beta_second * sec_ref[...] + (1.0 - beta_second) * grad_rot * grad_rot
    so_ref[...] = second
    direction = moment_rot / (jnp.sqrt(second) + epsilon)
    facing[:, 0:cols] = direction.astype(BF16)

    left_terms(facing[...], lb, bt)
    main = scatter_rows(bt, bt_core, bt_half, bt_full, bt_zs, bt_zr, bt_acc)
    next(main)
    run(swap)
    next(partner)
    run(main)
    next(factor, None)
    next(factor, None)
    back = jnp.concatenate([bt_acc[0], bt_acc[1]], axis=1).astype(BF16)
    back = jnp.concatenate([back, jnp.zeros((LANES - cols, 2 * LANES), BF16)], axis=0)

    for p in range(R):
        term = jnp.dot(rb[place(p)], back, preferred_element_type=F32).astype(BF16)
        for k in range(2):
            c = 2 * p + k
            for h in range(2):
                ut[c // X, c % X, h] = term[k * cols:(k + 1) * cols, h * LANES:(h + 1) * LANES]
    main = scatter_cols(ut, ut_half, ut_full, ut_zs, ut_za, ut_zb, ut_zt, ut_zc, ut_other, ut_acc)
    for k in range(14):
        next(main, None)
        for _ in range(FACTOR_AT.get(k, 0)):
            next(factor, None)
        for _ in range(PARTNER_AT.get(k, 0)):
            next(partner, None)
    run(factor, partner)
    left = jnp.zeros((rows, cols), F32)
    for p in range(R):
        left = left + lax.dot_general(
            pair(gb, p), jnp.concatenate([part[place(p)][0], part[place(p)][1]], axis=1),
            (((1,), (1,)), ((), ())), preferred_element_type=F32,
        )
    lo_ref[...] = beta_factor * lf_ref[...] + (1.0 - beta_factor) * left
    for h in range(2):
        half_rows = pl.ds(h * cols, cols)
        ro_ref[half_rows, :] = beta_factor * rf_ref[half_rows, :] + (1.0 - beta_factor) * turned_block(gt_acc[h])
    run(main)
    for h in range(2):
        up_ref[pl.ds(h * cols, cols), :] = turned_block(ut_acc[h]).astype(BF16)

    for condition, copy in pending:
        when(condition, copy.wait_send)


def per_device(dims, gradient, moment, second, left_factor, right_factor, left_basis_t, right_basis):
    ZH, Y, CORE, ZL, X = dims
    rows, cols = gradient.shape
    C = ZL * X

    def half_blocks(*lead, dtype=BF16):
        return pltpu.VMEM((*lead, 2, cols, LANES), dtype)

    def row_sum():
        return [
            half_blocks(CORE, ZH, Y), half_blocks(ZH, Y), pltpu.VMEM((ZH, 2, cols, LANES), BF16),
            half_blocks(ZH, 2), half_blocks(), half_blocks(), half_blocks(dtype=F32),
        ]

    block = jax.ShapeDtypeStruct((rows, cols), F32)
    return pl.pallas_call(
        functools.partial(kernel, dims),
        out_shape=(block, block, block, block, jax.ShapeDtypeStruct((rows, cols), BF16)),
        in_specs=[pl.BlockSpec(memory_space=pl.ANY)] * 7,
        out_specs=[pl.BlockSpec(memory_space=pltpu.VMEM)] * 5,
        scratch_shapes=[
            *(pltpu.VMEM((rows, cols), dtype) for dtype in (BF16, F32, F32, F32, F32, BF16, BF16)),
            *(pltpu.VMEM((C, rows, LANES), BF16) for _ in range(3)),
            *(pltpu.VMEM((CORE, ZH, Y, rows, LANES), BF16) for _ in range(3)),
            *row_sum(),
            *row_sum(),
            half_blocks(ZL, X), pltpu.VMEM((ZL, 2, cols, LANES), BF16), half_blocks(ZL, 2),
            half_blocks(ZL), half_blocks(ZL // 2), half_blocks(ZL // 2), half_blocks(), half_blocks(),
            half_blocks(dtype=F32), half_blocks(dtype=F32),
            half_blocks(CORE, ZH, Y),
            pltpu.VMEM((LANES, LANES), F32),
            pltpu.VMEM((rows, LANES), BF16),
            pltpu.SemaphoreType.DMA((320,)),
            pltpu.SemaphoreType.DMA((320,)),
            pltpu.SemaphoreType.DMA((7,)),
        ],
        compiler_params=pltpu.CompilerParams(
            collective_id=0, has_side_effects=True, vmem_limit_bytes=60 << 20
        ),
    )(gradient, moment, second, left_factor, right_factor, left_basis_t, right_basis)


def build(mesh, dims):
    placed = P("row", "col")
    return jax.shard_map(
        functools.partial(per_device, dims),
        mesh=mesh,
        in_specs=(placed,) * 7,
        out_specs=(placed,) * 5,
        check_vma=False,
    )


def solution(mesh):
    return build(mesh, DIMS)
```

```python
import functools

import jax
import jax.numpy as jnp
from jax import lax
from jax.experimental import pallas as pl
from jax.experimental.pallas import tpu as pltpu
from jax.sharding import PartitionSpec as P

beta_moment = 0.9
beta_second = 0.95
beta_factor = 0.95
epsilon = 1e-08

MESH = pl.DeviceIdType.MESH
LANES = 128
BF16 = jnp.bfloat16
F32 = jnp.float32
DIMS = (2, 4, 2, 8, 4)
LAG = 2
LEFT_FROM = 0
LEFT_EVERY = 2
FACTOR_AT = {0: 1, 4: 1, 10: 1}
PARTNER_AT = {0: 2, 4: 1, 5: 1, 8: 1, 9: 1, 12: 1}
RIGHT_AT = {3: 1, 9: 2, 11: 1, 12: 1, 13: 2}


def run(*steps):
    live = list(steps)
    while live:
        for one in list(live):
            try:
                next(one)
            except StopIteration:
                live.remove(one)


def both(first, second):
    if first is None:
        return second
    if second is None:
        return first
    return jnp.logical_and(first, second)


def when(condition, action):
    if condition is None:
        action()
    else:
        pl.when(condition)(action)


def kernel(
    dims, g_hbm, m_hbm, sec_hbm, lf_hbm, rf_hbm, l_hbm, r_hbm,
    lo_ref, ro_ref, mo_ref, so_ref, up_ref,
    g_ref, m_ref, sec_ref, lf_ref, rf_ref, l_ref, r_ref,
    gb, mb, lb, rb, hg, hm, bt, bt_core, bt_half, bt_full, bt_zs, bt_zr, bt_acc,
    gt, gt_core, gt_half, gt_full, gt_zs, gt_zr, gt_acc,
    ut, ut_half, ut_full, ut_zs, ut_za, ut_zb, ut_zt, ut_zc, ut_other, ut_acc, part, turn, facing,
    ssem, rsem, lsem,
):
    ZH, Y, CORE, ZL, X = dims
    R, C = ZH * Y * CORE, ZL * X
    rows, cols = g_ref.shape
    row, col = lax.axis_index("row"), lax.axis_index("col")
    core, y, zh = row % CORE, (row // CORE) % Y, row // (CORE * Y)
    x, z = col % X, col // X
    H = ZL // 2
    i, ours, there = z % H, z // H * H, (1 - z // H) * H

    def at_row(zh_, y_, core_):
        return ((zh_ * Y + y_) * CORE + core_, col)

    def at_col(z_, x_):
        return (row, z_ * X + x_)

    y_up, y_dn, y_far = (y + 1) % Y, (y + Y - 1) % Y, (y + 2) % Y
    x_up, x_dn, x_far = (x + 1) % X, (x + X - 1) % X, (x + 2) % X
    to_y_up, to_y_dn = at_row(zh, y_up, core), at_row(zh, y_dn, core)
    to_zh, to_core = at_row(1 - zh, y, core), at_row(zh, y, 1 - core)
    to_x_up, to_x_dn = at_col(z, x_up), at_col(z, x_dn)
    mirror = [(col // 2, 2 * row + e) for e in range(2)]
    mirror_core = (col // 2) % CORE
    mirror_y_zh = ((col // 2 // CORE) % Y, col // 2 // (CORE * Y))
    itself = [both(row == col // 2, col % 2 == e) for e in range(2)]
    to_z_up, to_z_dn = at_col(z + 1, x), at_col(z - 1, x)
    some = to_x_up if X > 1 else to_core if CORE > 1 else to_y_up

    counts = {"send": 0, "recv": 0}

    def sems(kind, number):
        first = counts[kind]
        counts[kind] += number
        return first

    pending = []

    def send(source, target, s, r, device, condition=None):
        copy = pltpu.make_async_remote_copy(
            src_ref=source, dst_ref=target, send_sem=ssem.at[s], recv_sem=rsem.at[r],
            device_id=device, device_id_type=MESH,
        )
        when(condition, copy.start)
        pending.append((condition, copy))

    def arrive(target, r, condition=None):
        copy = pltpu.make_async_remote_copy(
            src_ref=target, dst_ref=target, send_sem=ssem.at[0], recv_sem=rsem.at[r],
            device_id=some, device_id_type=MESH,
        )
        when(condition, copy.wait_recv)

    def gather_cols(buf):
        half = buf.shape[1] // 2
        low, high = pl.ds(0, half), pl.ds(half, half)
        lag = min(LAG, ZL)
        sz, rz = sems("send", 2 * ZL), sems("recv", ZL)
        sx, rx = sems("send", 4 * ZL), sems("recv", 4 * ZL)

        def slot(z_, x_):
            return z_ * X + x_

        def items(t):
            if t == 0:
                return [(z, None, 0)]
            return [(z - t, z >= t, 1), (z + t, z + t < ZL, -1)]

        def turn_corner(t):
            if X == 1:
                return
            for zo, ok, _ in items(t):
                arrive(buf.at[slot(zo, x_dn)], rx + 4 * zo, ok)
                send(buf.at[slot(zo, x_dn), low], buf.at[slot(zo, x_dn), low],
                     sx + 4 * zo + 2, rx + 4 * zo + 2, to_x_up, ok)
                arrive(buf.at[slot(zo, x_up)], rx + 4 * zo + 1, ok)
                send(buf.at[slot(zo, x_up), high], buf.at[slot(zo, x_up), high],
                     sx + 4 * zo + 3, rx + 4 * zo + 3, to_x_dn, ok)

        for t in range(ZL):
            for zo, ok, way in items(t):
                here = buf.at[slot(zo, x)]
                if t > 0:
                    arrive(here, rz + zo, ok)
                if way >= 0 and t < ZL - 1:
                    send(here, here, sz + zo, rz + zo, to_z_up, both(ok, z < ZL - 1))
                if way <= 0 and t < ZL - 1:
                    send(here, here, sz + ZL + zo, rz + zo, to_z_dn, both(ok, z > 0))
                if X > 1:
                    send(here, here, sx + 4 * zo, rx + 4 * zo, to_x_up, ok)
                    send(here, here, sx + 4 * zo + 1, rx + 4 * zo + 1, to_x_dn, ok)
            yield
            if t >= lag:
                turn_corner(t - lag)
                yield
        for t in range(ZL - lag, ZL):
            turn_corner(t)
            yield
        if X > 1:
            for zo in range(ZL):
                arrive(buf.at[slot(zo, x_far), low], rx + 4 * zo + 2)
                arrive(buf.at[slot(zo, x_far), high], rx + 4 * zo + 3)
            yield

    def gather_z(buf):
        sz, rz = sems("send", 2 * ZL), sems("recv", ZL)
        for t in range(ZL):
            ways = [(z, None, 0)] if t == 0 else [(z - t, z >= t, 1), (z + t, z + t < ZL, -1)]
            for zo, ok, way in ways:
                here = buf.at[zo * X + x]
                if t > 0:
                    arrive(here, rz + zo, ok)
                if way >= 0 and t < ZL - 1:
                    send(here, here, sz + zo, rz + zo, to_z_up, both(ok, z < ZL - 1))
                if way <= 0 and t < ZL - 1:
                    send(here, here, sz + ZL + zo, rz + zo, to_z_dn, both(ok, z > 0))
            yield

    def gather_x(buf):
        if X == 1:
            return
        half = buf.shape[1] // 2
        low, high = pl.ds(0, half), pl.ds(half, half)
        sx, rx = sems("send", 4 * ZL), sems("recv", 4 * ZL)
        for zo in range(ZL):
            here = buf.at[zo * X + x]
            send(here, here, sx + 4 * zo, rx + 4 * zo, to_x_up)
            send(here, here, sx + 4 * zo + 1, rx + 4 * zo + 1, to_x_dn)
        yield
        for zo in range(ZL):
            below, above = buf.at[zo * X + x_dn], buf.at[zo * X + x_up]
            arrive(below, rx + 4 * zo)
            send(below.at[low], below.at[low], sx + 4 * zo + 2, rx + 4 * zo + 2, to_x_up)
            arrive(above, rx + 4 * zo + 1)
            send(above.at[high], above.at[high], sx + 4 * zo + 3, rx + 4 * zo + 3, to_x_dn)
            if zo % 2 == 1:
                yield
        for zo in range(ZL):
            far = buf.at[zo * X + x_far]
            arrive(far.at[low], rx + 4 * zo + 2)
            arrive(far.at[high], rx + 4 * zo + 3)
        yield

    def gather_rows(buf):
        half = buf.shape[3] // 2
        low, high = pl.ds(0, half), pl.ds(half, half)
        sz, rz = sems("send", 1), sems("recv", 1)
        sy, ry = sems("send", 4 * ZH), sems("recv", 4 * ZH)
        sc, rc = sems("send", ZH), sems("recv", ZH)
        levels = [zh, 1 - zh][:ZH]
        here = buf.at[core, zh, y]
        if ZH > 1:
            send(here, here, sz, rz, to_zh)
        for k, zi in enumerate(levels):
            mine = buf.at[core, zi, y]
            if k == 1:
                yield
                arrive(mine, rz)
            if Y > 1:
                send(mine, mine, sy + 4 * k, ry + 4 * k, to_y_up)
                send(mine, mine, sy + 4 * k + 1, ry + 4 * k + 1, to_y_dn)
            if k == 0:
                yield
        yield
        for k, zi in enumerate(levels):
            if Y > 1:
                arrive(buf.at[core, zi, y_dn], ry + 4 * k)
                send(buf.at[core, zi, y_dn, low], buf.at[core, zi, y_dn, low],
                     sy + 4 * k + 2, ry + 4 * k + 2, to_y_up)
                arrive(buf.at[core, zi, y_up], ry + 4 * k + 1)
                send(buf.at[core, zi, y_up, high], buf.at[core, zi, y_up, high],
                     sy + 4 * k + 3, ry + 4 * k + 3, to_y_dn)
                yield
        for k, zi in enumerate(levels):
            if Y > 1:
                arrive(buf.at[core, zi, y_far, low], ry + 4 * k + 2)
                arrive(buf.at[core, zi, y_far, high], ry + 4 * k + 3)
            if CORE > 1:
                send(buf.at[core, zi], buf.at[core, zi], sc + k, rc + k, to_core)
            yield
        if CORE > 1:
            for k, zi in enumerate(levels):
                arrive(buf.at[1 - core, zi], rc + k)
            yield

    def add(target, value):
        target[...] = (target[...].astype(F32) + value[...].astype(F32)).astype(BF16)

    def scatter_rows(buf, from_core, halves, full, zs, zr, acc):
        sc, rc = sems("send", ZH), sems("recv", ZH)
        sy, ry = sems("send", 4 * ZH), sems("recv", 4 * ZH)
        sz, rz = sems("send", 1), sems("recv", 1)
        levels = [1 - zh, zh][-ZH:]
        if CORE > 1:
            for k, zi in enumerate(levels):
                send(buf.at[1 - core, zi], from_core.at[zi], sc + k, rc + k, to_core)
        yield
        for k, zi in enumerate(levels):
            if CORE > 1:
                arrive(from_core.at[zi], rc + k)
                add(buf.at[core, zi], from_core.at[zi])
            if Y > 1:
                send(buf.at[core, zi, y_far, 0], halves.at[zi, 0], sy + 4 * k, ry + 4 * k, to_y_up)
                send(buf.at[core, zi, y_far, 1], halves.at[zi, 1], sy + 4 * k + 1, ry + 4 * k + 1, to_y_dn)
            yield
        for k, zi in enumerate(levels):
            if Y > 1:
                arrive(halves.at[zi, 0], ry + 4 * k)
                add(buf.at[core, zi, y_up, 0], halves.at[zi, 0])
                send(buf.at[core, zi, y_up], full.at[zi, 0], sy + 4 * k + 2, ry + 4 * k + 2, to_y_up)
                arrive(halves.at[zi, 1], ry + 4 * k + 1)
                add(buf.at[core, zi, y_dn, 1], halves.at[zi, 1])
                send(buf.at[core, zi, y_dn], full.at[zi, 1], sy + 4 * k + 3, ry + 4 * k + 3, to_y_dn)
                yield
        for k, zi in enumerate(levels):
            total = buf[core, zi, y].astype(F32)
            if Y > 1:
                arrive(full.at[zi, 0], ry + 4 * k + 2)
                arrive(full.at[zi, 1], ry + 4 * k + 3)
                total = total + full[zi, 0].astype(F32) + full[zi, 1].astype(F32)
            if ZH > 1 and k == 0:
                zs[...] = total.astype(BF16)
                send(zs, zr, sz, rz, to_zh)
            else:
                acc[...] = total
            yield
        if ZH > 1:
            arrive(zr, rz)
            acc[...] = acc[...] + zr[...].astype(F32)
            yield

    def scatter_cols(buf, halves, full, zs, za, zb, zt, zc, other, acc):
        sx, rx = sems("send", 4 * ZL), sems("recv", 4 * ZL)
        sz, ra, rb_ = sems("send", ZL), sems("recv", H), sems("recv", H)
        sc, rc = sems("send", 1), sems("recv", 1)
        order = [there + j for j in range(H)] + [ours + j for j in range(H)]
        if X > 1:
            for k, d in enumerate(order):
                send(buf.at[d, x_far, 0], halves.at[k, 0], sx + 4 * k, rx + 4 * k, to_x_up)
                send(buf.at[d, x_far, 1], halves.at[k, 1], sx + 4 * k + 1, rx + 4 * k + 1, to_x_dn)
        yield

        def along(k):
            d, j = order[k], k % H
            total = buf[d, x].astype(F32)
            if X > 1:
                arrive(full.at[k, 0], rx + 4 * k + 2)
                arrive(full.at[k, 1], rx + 4 * k + 3)
                total = total + full[k, 0].astype(F32) + full[k, 1].astype(F32)
            zs[k] = total.astype(BF16)
            target, keep, r = (za, other, ra) if k < H else (zb, acc, rb_)
            send(zs.at[k], target.at[i], sz + k, r + i, at_col(ours + j, x), i != j)

            @pl.when(i == j)
            def _():
                keep[...] = total

        def gathered(source, r, into):
            for j in range(H):
                @pl.when(i != j)
                def _():
                    arrive(source.at[j], r + j)
                    into[...] = into[...] + source[j].astype(F32)

        lag = min(2, ZL - 1)
        for k in range(ZL + lag):
            if k < ZL and X > 1:
                d = order[k]
                arrive(halves.at[k, 0], rx + 4 * k)
                add(buf.at[d, x_up, 0], halves.at[k, 0])
                send(buf.at[d, x_up], full.at[k, 0], sx + 4 * k + 2, rx + 4 * k + 2, to_x_up)
                arrive(halves.at[k, 1], rx + 4 * k + 1)
                add(buf.at[d, x_dn, 1], halves.at[k, 1])
                send(buf.at[d, x_dn], full.at[k, 1], sx + 4 * k + 3, rx + 4 * k + 3, to_x_dn)
                yield
            if k >= lag:
                along(k - lag)
                yield
            if k - lag == min(H + 1, ZL - 1):
                gathered(za, ra, other)
                zt[...] = other[...].astype(BF16)
                send(zt, zc, sc, rc, at_col(there + i, x))
                yield
        gathered(zb, rb_, acc)
        arrive(zc, rc)
        acc[...] = acc[...] + zc[...].astype(F32)
        yield

    def exchange():
        sx, rx = sems("send", 2), sems("recv", 2)
        own_place = part.at[core, zh, y]
        for e in range(2):
            send(gb.at[col, pl.ds(e * cols, cols)], part.at[mirror_core, mirror_y_zh[1], mirror_y_zh[0], col % 2],
                 sx + e, rx + col % 2, mirror[e], jnp.logical_not(itself[e]))

            @pl.when(itself[e])
            def _():
                part[core, zh, y, e] = gb[col, e * cols:(e + 1) * cols, :]

        yield
        for e in range(2):
            arrive(own_place.at[e], rx + e, jnp.logical_not(itself[e]))

    def place(p):
        return p % CORE, p // (CORE * Y), (p // CORE) % Y

    def spread(block):
        pad = jnp.zeros((LANES - cols, block.shape[1]), block.dtype)
        return jnp.concatenate([block[:cols], pad, block[cols:], pad], axis=0)

    def pair(buf, p):
        return jnp.concatenate([buf[2 * p], buf[2 * p + 1]], axis=1)

    def left_terms(side, buf, target):
        turned = side.astype(F32).T.astype(BF16)
        for p in range(R):
            term = jnp.dot(turned, pair(buf, p), preferred_element_type=F32)[:cols].astype(BF16)
            c, h, j = place(p)
            target[c, h, j, 0] = term[:, :LANES]
            target[c, h, j, 1] = term[:, LANES:]

    def turned_block(acc):
        turn[0:cols, :] = acc
        return turn[...].T[:cols, :cols]

    loads = [
        pltpu.make_async_copy(source, target, lsem.at[n])
        for n, (source, target) in enumerate((
            (g_hbm, g_ref), (m_hbm, m_ref), (r_hbm, r_ref), (l_hbm, l_ref),
            (sec_hbm, sec_ref), (lf_hbm, lf_ref), (rf_hbm, rf_ref),
        ))
    ]
    for load in loads:
        load.start()

    barrier = pltpu.get_barrier_semaphore()

    def greet(device):
        pl.semaphore_signal(barrier, inc=1, device_id=device, device_id_type=MESH)

    greeted = 0
    for present, devices in (
        (ZH > 1, (to_zh,)), (CORE > 1, (to_core,)), (Y > 1, (to_y_up, to_y_dn)), (X > 1, (to_x_up, to_x_dn)),
        (True, (at_col(there + i, x),)),
    ):
        if present:
            for device in devices:
                greet(device)
                greeted += 1
    for j in range(H):
        pl.when(i != j)(functools.partial(greet, at_col(ours + j, x)))
    greeted += H - 1
    edge = jnp.logical_or(z == H - 1, z == H)
    if H > 1:
        pl.when(z == H - 1)(lambda: greet(to_z_up))
        pl.when(z == H)(lambda: greet(to_z_dn))

    for e in range(2):
        pl.when(jnp.logical_not(itself[e]))(functools.partial(greet, mirror[e]))
    expected = greeted + jnp.where(row == col // 2, 1, 2)
    if H > 1:
        expected = expected + jnp.where(edge, 1, 0)

    gb[col] = jnp.zeros(gb.shape[1:], BF16)
    mb[col] = jnp.zeros(mb.shape[1:], BF16)
    lb[col] = jnp.zeros(lb.shape[1:], BF16)
    rb[core, zh, y] = jnp.zeros(rb.shape[3:], BF16)
    facing[...] = jnp.zeros(facing.shape, BF16)
    turn[...] = jnp.zeros(turn.shape, F32)
    for load in loads[:4]:
        load.wait()
    g = g_ref[...]
    moment = beta_moment * m_ref[...] + (1.0 - beta_moment) * g.astype(F32)
    mo_ref[...] = moment
    gb[col, :, 0:cols] = g
    mb[col, :, 0:cols] = moment.astype(BF16)
    lb[col, :, 0:cols] = l_ref[...]
    rb[core, zh, y, :, 0:cols] = r_ref[...]

    pl.semaphore_wait(barrier, expected)

    def rotate(source, target):
        rotated = jnp.zeros((rows, LANES), F32)
        for p in range(R):
            rotated = rotated + jnp.dot(pair(source, p), spread(rb[place(p)]), preferred_element_type=F32)
        target[core, zh, y] = rotated.astype(BF16)

    factor = scatter_rows(gt, gt_core, gt_half, gt_full, gt_zs, gt_zr, gt_acc)
    swap, partner = exchange(), gather_rows(part)
    left_z, left_x = gather_z(lb), gather_x(lb)
    grad_cols, moment_cols, right_rows = gather_cols(gb), gather_cols(mb), gather_rows(rb)
    for k in range(14):
        next(grad_cols, None)
        next(moment_cols, None)
        for _ in range(RIGHT_AT.get(k, 0)):
            next(right_rows, None)
        if k >= LEFT_FROM and (k - LEFT_FROM) % LEFT_EVERY == 0:
            next(left_z, None)
    run(grad_cols, moment_cols, right_rows)
    rotate(gb, hg)
    grad_rows, moment_rows = gather_rows(hg), gather_rows(hm)
    next(grad_rows)
    rotate(mb, hm)
    next(moment_rows)
    run(left_z)
    next(left_x, None)
    next(swap)
    left_terms(gb[col], gb, gt)
    next(factor)
    run(grad_rows, moment_rows, left_x)
    next(factor)
    next(factor)
    for load in loads[4:]:
        load.wait()
    rot = jnp.zeros((rows, 2 * LANES), F32)
    for p in range(R):
        both_rotated = jnp.concatenate([spread(hg[place(p)]), spread(hm[place(p)])], axis=1)
        rot = rot + jnp.dot(pair(lb, p), both_rotated, preferred_element_type=F32)
    grad_rot, moment_rot = rot[:, 0:cols], rot[:, LANES:LANES + cols]
    second = beta_second * sec_ref[...] + (1.0 - beta_second) * grad_rot * grad_rot
    so_ref[...] = second
    direction = moment_rot / (jnp.sqrt(second) + epsilon)
    facing[:, 0:cols] = direction.astype(BF16)

    left_terms(facing[...], lb, bt)
    main = scatter_rows(bt, bt_core, bt_half, bt_full, bt_zs, bt_zr, bt_acc)
    next(main)
    run(swap)
    next(partner)
    run(main)
    next(factor, None)
    next(factor, None)
    back = jnp.concatenate([bt_acc[0], bt_acc[1]], axis=1).astype(BF16)
    back = jnp.concatenate([back, jnp.zeros((LANES - cols, 2 * LANES), BF16)], axis=0)

    for p in range(R):
        term = jnp.dot(rb[place(p)], back, preferred_element_type=F32).astype(BF16)
        for k in range(2):
            c = 2 * p + k
            for h in range(2):
                ut[c // X, c % X, h] = term[k * cols:(k + 1) * cols, h * LANES:(h + 1) * LANES]
    main = scatter_cols(ut, ut_half, ut_full, ut_zs, ut_za, ut_zb, ut_zt, ut_zc, ut_other, ut_acc)
    for k in range(18):
        next(main, None)
        for _ in range(FACTOR_AT.get(k, 0)):
            next(factor, None)
        for _ in range(PARTNER_AT.get(k, 0)):
            next(partner, None)
    run(factor, partner)
    left = jnp.zeros((rows, cols), F32)
    for p in range(R):
        left = left + lax.dot_general(
            pair(gb, p), jnp.concatenate([part[place(p)][0], part[place(p)][1]], axis=1),
            (((1,), (1,)), ((), ())), preferred_element_type=F32,
        )
    lo_ref[...] = beta_factor * lf_ref[...] + (1.0 - beta_factor) * left
    for h in range(2):
        half_rows = pl.ds(h * cols, cols)
        ro_ref[half_rows, :] = beta_factor * rf_ref[half_rows, :] + (1.0 - beta_factor) * turned_block(gt_acc[h])
    run(main)
    for h in range(2):
        up_ref[pl.ds(h * cols, cols), :] = turned_block(ut_acc[h]).astype(BF16)

    for condition, copy in pending:
        when(condition, copy.wait_send)


def per_device(dims, gradient, moment, second, left_factor, right_factor, left_basis_t, right_basis):
    ZH, Y, CORE, ZL, X = dims
    rows, cols = gradient.shape
    C = ZL * X

    def half_blocks(*lead, dtype=BF16):
        return pltpu.VMEM((*lead, 2, cols, LANES), dtype)

    def row_sum():
        return [
            half_blocks(CORE, ZH, Y), half_blocks(ZH, Y), pltpu.VMEM((ZH, 2, cols, LANES), BF16),
            half_blocks(ZH, 2), half_blocks(), half_blocks(), half_blocks(dtype=F32),
        ]

    block = jax.ShapeDtypeStruct((rows, cols), F32)
    return pl.pallas_call(
        functools.partial(kernel, dims),
        out_shape=(block, block, block, block, jax.ShapeDtypeStruct((rows, cols), BF16)),
        in_specs=[pl.BlockSpec(memory_space=pl.ANY)] * 7,
        out_specs=[pl.BlockSpec(memory_space=pltpu.VMEM)] * 5,
        scratch_shapes=[
            *(pltpu.VMEM((rows, cols), dtype) for dtype in (BF16, F32, F32, F32, F32, BF16, BF16)),
            *(pltpu.VMEM((C, rows, LANES), BF16) for _ in range(3)),
            *(pltpu.VMEM((CORE, ZH, Y, rows, LANES), BF16) for _ in range(3)),
            *row_sum(),
            *row_sum(),
            half_blocks(ZL, X), pltpu.VMEM((ZL, 2, cols, LANES), BF16), half_blocks(ZL, 2),
            half_blocks(ZL), half_blocks(ZL // 2), half_blocks(ZL // 2), half_blocks(), half_blocks(),
            half_blocks(dtype=F32), half_blocks(dtype=F32),
            half_blocks(CORE, ZH, Y),
            pltpu.VMEM((LANES, LANES), F32),
            pltpu.VMEM((rows, LANES), BF16),
            pltpu.SemaphoreType.DMA((320,)),
            pltpu.SemaphoreType.DMA((320,)),
            pltpu.SemaphoreType.DMA((7,)),
        ],
        compiler_params=pltpu.CompilerParams(
            collective_id=0, has_side_effects=True, vmem_limit_bytes=60 << 20
        ),
    )(gradient, moment, second, left_factor, right_factor, left_basis_t, right_basis)


def build(mesh, dims):
    placed = P("row", "col")
    return jax.shard_map(
        functools.partial(per_device, dims),
        mesh=mesh,
        in_specs=(placed,) * 7,
        out_specs=(placed,) * 5,
        check_vma=False,
    )


def solution(mesh):
    return build(mesh, DIMS)
```
